32 devices in a mesh: wide: 16 (over z, x, core), narrow: 2 (over y).
Axes of the slice: x: 2, y: 2, z: 4, core: 2. Of those that a mesh axis runs over, the one named last changes fastest.
Arguments:
- amplitudes: bfloat16 [2048, 2048], P(('wide', 'narrow')), may hold values from -6 to 6
- amp_mask: int32 [32, 32], replicated, may hold values from 0 to 1, as said below
- integrals: bfloat16 [2048, 8192], P('narrow', 'wide'), may hold values from -0.59765625 to 0.59765625
- int_mask: int32 [32, 128], replicated, may hold values from 0 to 1, as said below
- owner: int32 [128], replicated, may hold values from 0 to 127, each once
- occ_energy: float32 [2048], P('narrow'), may hold values from -3 to -0.5
- vir_energy: float32 [8192], replicated, may hold values from 1 to 8
Outputs:
- update: bfloat16 [2048, 8192], P('narrow', 'wide')
The draws below stay inside these ranges and needn't reach their ends.
Inputs may be any that keep to these rules, and one draw needn't show every extreme that they name: `amp_mask`: 1 marks a pair of tiles within the screening distance, 0 one outside it. `int_mask`: 1 marks a pair of tiles within the screening distance, 0 one outside it. A permutation of the 128 tiles; columns 64 * s to 64 * s + 63 of integrals and update belong to tile owner[s].
All inputs are finite; a program needn't handle non-finite values.
Results may differ from the reference program's by a relative error of at most 0.001.
Values may be sent and summed in bfloat16 or wider, within the bound.
A program may use at most 64 MiB of HBM per device.

```python
import jax
import jax.numpy as jnp
from jax import lax

TILE = 64
K_TILES = 32
Q_DEV = 512
K = 2048
OP = 2048
Q = 8192
OP_TILES = 32
Q_TILES = 128
N_WIDE = 16


span_units = 1024


reach_units = 256


def tile_positions(key):
    vir_pos = jax.random.randint(jax.random.fold_in(key, 11), (K_TILES,), 0, span_units)
    occ_base = jnp.arange(OP_TILES, dtype=jnp.int32) * span_units // OP_TILES
    occ_pos = occ_base + jax.random.randint(jax.random.fold_in(key, 12), (OP_TILES,), 0, max(span_units // OP_TILES, 1))
    out_pos = jax.random.randint(jax.random.fold_in(key, 13), (Q_TILES,), 0, span_units)
    return (vir_pos, occ_pos, out_pos)


def draw_amp_mask(key, part):
    vir_pos, occ_pos, out_pos = tile_positions(key)
    return jnp.where(jnp.abs(vir_pos[:, None] - occ_pos[None, :]) <= reach_units, 1, 0).astype(jnp.int32)


def draw_int_mask(key, part):
    vir_pos, occ_pos, out_pos = tile_positions(key)
    return jnp.where(jnp.abs(vir_pos[:, None] - out_pos[None, :]) <= reach_units, 1, 0).astype(jnp.int32)


def shard_levels(stream_key, shape, shards, low, top_value):
    factor_of, own = 1.0, jax.random.fold_in(stream_key, 6)
    for position, parts in shards:
        heights = jnp.exp(jax.random.uniform(jax.random.fold_in(own, position), (parts,), jnp.float32, low / len(shards), top_value / len(shards)))
        factor_of = factor_of * jnp.repeat(heights, shape[position] // parts).reshape([-1 if axis == position else 1 for axis in range(len(shape))])
    return factor_of


def bell_draw(own_key, extent, spread, most, pieces=(), kind=jnp.bfloat16):
    values = jax.random.normal(own_key, extent, jnp.float32) * spread
    if len(pieces) > 0:
        values = shard_levels(own_key, extent, pieces, -0.22, 0.18) * values
    return jnp.clip(values, min=-most, max=most).astype(kind)


def setup_inputs(seed: int = 0) -> dict:
    key_of = jax.random.split(jax.random.key(seed), 8)
    return {
        "amplitudes": bell_draw(key_of[0], (K, OP), 1.0, 6.0, ((0, 32),)),
        "amp_mask": draw_amp_mask(jax.random.fold_in(key_of[7], 71), 0),
        "integrals": bell_draw(key_of[2], (K, Q), 0.1, 0.59765625, ((0, 2), (1, 16))),
        "int_mask": draw_int_mask(jax.random.fold_in(key_of[7], 71), 0),
        "owner": jax.random.permutation(key_of[4], Q_TILES).astype(jnp.int32),
        "occ_energy": jnp.clip(-3.0 + 2.5 * jax.random.uniform(key_of[5], (OP,), jnp.float32) ** shard_levels(key_of[5], (OP,), ((0, 2),), -0.2, 0.2), -3.0, -0.5),
        "vir_energy": jnp.clip(jax.random.uniform(key_of[6], (Q,), jnp.float32, 1.0, 8.0), 1.0, 8.0),
    }


def reference(amplitudes, amp_mask, integrals, int_mask, owner, occ_energy, vir_energy):
    amp_wide = jnp.repeat(jnp.repeat(amp_mask, TILE, axis=0), TILE, axis=1)
    masked = jnp.where(amp_wide == 1, amplitudes, jnp.zeros((), amplitudes.dtype))
    amp_trans = masked.T
    per_block = Q_DEV // TILE
    vir_tiles = vir_energy.reshape(Q_TILES, TILE)

    def one_block(block_index):
        slot_ids = block_index * per_block + jnp.arange(per_block, dtype=jnp.int32)
        tile_ids = owner[slot_ids]
        col_mask = jnp.repeat(jnp.repeat(int_mask[:, tile_ids], TILE, axis=0), TILE, axis=1)
        int_panel = lax.dynamic_slice_in_dim(integrals, (block_index * Q_DEV).astype(jnp.int32), Q_DEV, 1)
        int_panel = jnp.where(col_mask == 1, int_panel, jnp.zeros((), integrals.dtype))
        ladder = jnp.dot(amp_trans, int_panel, preferred_element_type=jnp.float32)
        energy = vir_tiles[tile_ids].reshape(Q_DEV)
        denominator = energy[None, :] - occ_energy[:, None]
        return (ladder / denominator).astype(jnp.bfloat16)

    blocks = lax.map(one_block, jnp.arange(N_WIDE, dtype=jnp.int32))
    return blocks.transpose(1, 0, 2).reshape(OP, Q)
```

```python
import functools

import jax
import jax.numpy as jnp
from jax import lax
from jax.experimental import pallas as pl
from jax.experimental.pallas import tpu as pltpu
from jax.sharding import PartitionSpec as P

TILE = 64


def contract_rows(summed, rows_in, int_part):
    return summed + lax.dot_general(
        rows_in, int_part, (((0,), (0,)), ((), ())), preferred_element_type=jnp.float32
    )


def contract_all(amp_full, int_full, starting):
    k_total = amp_full.shape[0]
    block_rows = min(512, k_total)
    summed = starting
    for first_row in range(0, k_total, block_rows):
        summed = contract_rows(
            summed,
            amp_full[first_row : first_row + block_rows],
            int_full[first_row : first_row + block_rows],
        )
    return summed


def shards(amplitudes, amp_mask, integrals, int_mask, owner, occ_energy, vir_energy):
    tile_width = TILE
    narrow_count = lax.axis_size("narrow")
    wide_index = lax.axis_index("wide")
    narrow_index = lax.axis_index("narrow")
    src_rows = amplitudes.shape[0]
    occ_all = amplitudes.shape[1]
    occ_here = occ_energy.shape[0]
    vir_here = integrals.shape[1]
    first_src = (wide_index * narrow_count + narrow_index) * src_rows
    src_tiles = (first_src + jnp.arange(src_rows, dtype=jnp.int32)) // tile_width
    src_mask = jnp.take(amp_mask, src_tiles, axis=0)
    src_wide = jnp.broadcast_to(
        src_mask[:, :, None], (src_rows, occ_all // tile_width, tile_width)
    ).reshape(src_rows, occ_all)
    masked = jnp.where(src_wide == 1, amplitudes, jnp.zeros((), amplitudes.dtype))
    vir_tiles_here = vir_here // tile_width
    slot_ids = wide_index * vir_tiles_here + jnp.arange(vir_tiles_here, dtype=jnp.int32)
    tile_ids = jnp.take(owner, slot_ids)
    vir_mask = jnp.take(int_mask, tile_ids, axis=1)
    int_rows = integrals.shape[0]
    row_tiles = int_rows // tile_width
    local_mask = lax.dynamic_slice_in_dim(vir_mask, narrow_index * row_tiles, row_tiles, 0)
    local_wide = jnp.broadcast_to(
        local_mask[:, None, :, None], (row_tiles, tile_width, vir_tiles_here, tile_width)
    ).reshape(int_rows, vir_here)
    int_masked = jnp.where(local_wide == 1, integrals, jnp.zeros((), integrals.dtype))
    int_full = lax.all_gather(int_masked, "narrow", axis=0, tiled=True)
    starting = jnp.zeros((occ_here, vir_here), jnp.float32)
    regrouped = lax.all_to_all(masked, "narrow", split_axis=1, concat_axis=0, tiled=True)
    amp_full = lax.all_gather(regrouped, "wide", axis=0, tiled=True)
    ladder = contract_all(amp_full, int_full, starting)
    vir_energy_here = jnp.take(vir_energy.reshape(-1, tile_width), tile_ids, axis=0).reshape(
        vir_here
    )
    denominator = vir_energy_here[None, :] - occ_energy[:, None]
    return (ladder / denominator).astype(jnp.bfloat16)


MESH = pl.DeviceIdType.MESH
LANES = 128


def lookup(table, z, y):
    value = jnp.int32(table[0][0])
    for zz in range(len(table)):
        for yy in range(2):
            value = jnp.where((z == zz) & (y == yy), jnp.int32(table[zz][yy]), value)
    return value


def schedule(z_count):
    half = z_count // 2
    orders, sends = [], []
    for z in range(z_count):
        row, send = [], []
        for y in range(2):
            remote = sorted(range((1 - y) * half, (2 - y) * half), key=lambda g: abs(g - z))
            near = sorted((g for g in range(z_count) if g != remote[-1]), key=lambda g: abs(g - z))
            row.append(near + [remote[-1]])
            send.append(sorted(range(y * half, (y + 1) * half), key=lambda g: abs(g - z)))
        orders.append(row)
        sends.append(send)
    return orders, sends


def ladder_kernel(
    z_count,
    amp_hbm,
    int_hbm,
    amask_ref,
    imask_ref,
    owner_ref,
    occ_ref,
    vir_ref,
    out_hbm,
    amp_scr,
    int_scr,
    acc,
    recip,
    amask,
    imask,
    out_scr,
    occ_cols,
    own_sem,
    ycross_send,
    int_send,
    int_recv,
    send_sem,
    recv_sem,
    out_sem,
):
    w = lax.axis_index("wide")
    y = lax.axis_index("narrow")
    z, x, c = w // 4, (w // 2) % 2, w % 2
    rows = amp_hbm.shape[0]
    occ_here, vir_here = acc.shape
    group = int_scr.shape[0] // z_count
    half_groups = z_count // 2
    orders, sends = schedule(z_count)

    def wide_id(zz, xx, cc):
        return zz * 4 + xx * 2 + cc

    y_peer = (w, 1 - y)
    x_peer = (wide_id(z, 1 - x, c), y)
    c_peer = (wide_id(z, x, 1 - c), y)
    r_peer = (w + 4, y)
    l_peer = (w - 4, y)
    has_r, has_l = z < z_count - 1, z > 0

    barrier = pltpu.get_barrier_semaphore()
    for peer in (y_peer, x_peer, c_peer):
        pl.semaphore_signal(barrier, inc=1, device_id=peer, device_id_type=MESH)

    @pl.when(has_r)
    def _():
        pl.semaphore_signal(barrier, inc=1, device_id=r_peer, device_id_type=MESH)

    @pl.when(has_l)
    def _():
        pl.semaphore_signal(barrier, inc=1, device_id=l_peer, device_id_type=MESH)

    pl.semaphore_wait(barrier, 3 + jnp.where(has_r, 1, 0) + jnp.where(has_l, 1, 0))

    def block_id(zz, xx, cc, h):
        return wide_id(zz, xx, cc) * 2 + h

    def block(zz, xx, cc, h):
        first = pl.multiple_of(block_id(zz, xx, cc, h) * rows, rows)
        return amp_scr.at[pl.ds(first, rows), :]

    def half_cols(yy):
        return amp_hbm.at[:, pl.ds(pl.multiple_of(yy * occ_here, LANES), occ_here)]

    RIGHT, LEFT, ACROSS, CORE, CORE2 = range(5)
    peers = (r_peer, l_peer, x_peer, c_peer, c_peer)

    def copy(kind, zz, xx, h, src=None):
        there = block(zz, xx, c, h)
        return pltpu.make_async_remote_copy(
            src_ref=there if src is None else src,
            dst_ref=there,
            send_sem=send_sem.at[kind, zz * 2 + h],
            recv_sem=recv_sem.at[block_id(zz, xx, c, h)],
            device_id=peers[kind],
            device_id_type=MESH,
        )

    def arrived(zz, xx, cc, h):
        here = block(zz, xx, cc, h)
        pltpu.make_async_remote_copy(
            src_ref=here,
            dst_ref=here,
            send_sem=send_sem.at[CORE, zz * 2 + h],
            recv_sem=recv_sem.at[block_id(zz, xx, cc, h)],
            device_id=c_peer,
            device_id_type=MESH,
        ).wait_recv()

    cross = pltpu.make_async_remote_copy(
        src_ref=half_cols(1 - y),
        dst_ref=block(z, x, c, y),
        send_sem=ycross_send,
        recv_sem=recv_sem.at[block_id(z, x, c, y)],
        device_id=y_peer,
        device_id_type=MESH,
    )
    cross.start()

    def spread_own(h, src):
        @pl.when(has_r)
        def _():
            copy(RIGHT, z, x, h, src).start()

        @pl.when(has_l)
        def _():
            copy(LEFT, z, x, h, src).start()

        copy(ACROSS, z, x, h, src).start()
        copy(CORE, z, x, h, src).start()

    spread_own(y, half_cols(y))

    def int_rows(g):
        return int_scr.at[pl.ds(pl.multiple_of(g * group, group), group), :]

    def int_local(g):
        first = pl.multiple_of((g - y * half_groups) * group, group)
        return int_hbm.at[pl.ds(first, group), :]

    def int_copy(g):
        return pltpu.make_async_remote_copy(
            src_ref=int_local(g),
            dst_ref=int_rows(g),
            send_sem=int_send.at[g],
            recv_sem=int_recv.at[g],
            device_id=y_peer,
            device_id_type=MESH,
        )

    for i in range(half_groups):
        int_copy(lookup([[r[i] for r in row] for row in sends], z, y)).start()

    own_copy = pltpu.make_async_copy(half_cols(y), block(z, x, c, y), own_sem.at[0])
    own_copy.start()
    held = pltpu.make_async_copy(
        int_hbm,
        int_scr.at[
            pl.ds(pl.multiple_of(y * half_groups * group, group), half_groups * group), :
        ],
        own_sem.at[1],
    )
    held.start()

    slots = vir_here // TILE
    lane = lax.broadcasted_iota(jnp.int32, (1, vir_here), 1) // TILE
    tile_of = jnp.zeros((1, vir_here), jnp.int32)
    for j in range(slots):
        tile_of = jnp.where(lane == j, owner_ref[w * slots + j], tile_of)
    q_tiles = imask_ref.shape[1]
    pick = lax.broadcasted_iota(jnp.int32, (q_tiles, vir_here), 0) == tile_of
    imask[...] = jnp.dot(
        imask_ref[...].astype(jnp.float32).astype(jnp.bfloat16),
        jnp.where(pick, 1.0, 0.0).astype(jnp.bfloat16),
        preferred_element_type=jnp.float32,
    )
    p_tiles = amask_ref.shape[1]
    p_tile = y * (occ_here // TILE) + lax.broadcasted_iota(jnp.int32, (p_tiles, occ_here), 1) // TILE
    pick_p = lax.broadcasted_iota(jnp.int32, (p_tiles, occ_here), 0) == p_tile
    amask[...] = jnp.dot(
        amask_ref[...].astype(jnp.float32).astype(jnp.bfloat16),
        jnp.where(pick_p, 1.0, 0.0).astype(jnp.bfloat16),
        preferred_element_type=jnp.float32,
    )

    arrived(z, x, c, 1 - y)
    spread_own(1 - y, block(z, x, c, 1 - y))

    low = lax.broadcasted_iota(jnp.int32, (1, LANES), 1) < TILE

    def energies(tile, upper):
        row = vir_ref[pl.ds(tile // 2, 1), :]
        turned = jnp.concatenate([row[:, TILE:], row[:, :TILE]], axis=1)
        odd = jnp.full((1, LANES), tile % 2, jnp.int32) == upper
        return jnp.where(odd, row, turned)

    occ_t = jnp.transpose(occ_ref[...])
    for j in range(occ_here // LANES):
        occ_cols[j * LANES : (j + 1) * LANES, :] = jnp.broadcast_to(
            occ_t[:, j : j + 1], (LANES, LANES)
        )
    for j in range(slots // 2):
        first = energies(owner_ref[w * slots + 2 * j], 0)
        second = energies(owner_ref[w * slots + 2 * j + 1], 1)
        vir_row = jnp.where(low, first, second)

        @pl.loop(0, occ_here // LANES)
        def _(i):
            at = pl.ds(pl.multiple_of(i * LANES, LANES), LANES)
            recip[at, j * LANES : (j + 1) * LANES] = 1.0 / (vir_row - occ_cols[at, :])

    step = 256

    def masked_integrals(g):
        @pl.when(g // half_groups != y)
        def _():
            pltpu.make_async_remote_copy(
                src_ref=int_rows(g),
                dst_ref=int_rows(g),
                send_sem=int_send.at[g],
                recv_sem=int_recv.at[g],
                device_id=y_peer,
                device_id_type=MESH,
            ).wait_recv()

        for t in range(group // TILE):
            at = pl.ds(pl.multiple_of(g * group + t * TILE, TILE), TILE)
            row = imask[pl.ds(g * (group // TILE) + t, 1), :].astype(jnp.bfloat16)
            int_scr[at, :] = int_scr[at, :] * jnp.broadcast_to(row, (TILE, vir_here))

    def multiply(g, first, last):
        masked_integrals(g)

        @pl.loop(0, occ_here // step)
        def _(i):
            cols = pl.ds(pl.multiple_of(i * step, step), step)
            parts = []
            for t in range(group // TILE):
                at = pl.ds(pl.multiple_of(g * group + t * TILE, TILE), TILE)
                row = amask[pl.ds(g * (group // TILE) + t, 1), cols].astype(jnp.bfloat16)
                parts.append(amp_scr[at, cols] * jnp.broadcast_to(row, (TILE, step)))
            left = jnp.concatenate(parts, axis=0)
            here = pl.ds(pl.multiple_of(g * group, group), group)
            term = lax.dot_general(
                left, int_scr[here, :], (((0,), (0,)), ((), ())),
                preferred_element_type=jnp.float32,
            )
            if first:
                acc[cols, :] = term
            elif not last:
                acc[cols, :] += term
            else:
                out_scr[cols, :] = ((acc[cols, :] + term) * recip[cols, :]).astype(jnp.bfloat16)
                pltpu.make_async_copy(
                    out_scr.at[cols, :], out_hbm.at[cols, :], out_sem.at[i]
                ).start()

    def on_left(s, act):
        @pl.when(z - s >= 0)
        def _():
            act(z - s)

    def on_right(s, act):
        @pl.when(z + s <= z_count - 1)
        def _():
            act(z + s)

    def x_arrivals(s):
        for h in (y, 1 - y):

            def act(zz):
                arrived(zz, 1 - x, c, h)
                copy(CORE2, zz, 1 - x, h).start()

            if s == 0:
                act(z)
            else:
                on_left(s, act)
                on_right(s, act)

    for s in range(1, z_count):
        for h in (y, 1 - y):

            def from_left(zz):
                arrived(zz, x, c, h)

                @pl.when(has_r)
                def _():
                    copy(RIGHT, zz, x, h).start()

                copy(ACROSS, zz, x, h).start()
                copy(CORE, zz, x, h).start()

            def from_right(zz):
                arrived(zz, x, c, h)

                @pl.when(has_l)
                def _():
                    copy(LEFT, zz, x, h).start()

                copy(ACROSS, zz, x, h).start()
                copy(CORE, zz, x, h).start()

            on_left(s, from_left)
            on_right(s, from_right)
        x_arrivals(s - 1)

    own_copy.wait()
    held.wait()

    def core_arrivals(g):
        for xx in range(2):
            for h in range(2):
                arrived(g, xx, 1 - c, h)

    group_at = [lookup([[r[i] for r in row] for row in orders], z, y) for i in range(z_count)]
    for i in range(z_count):
        if i == half_groups:
            x_arrivals(z_count - 1)
        core_arrivals(group_at[i])
        multiply(group_at[i], i == 0, i == z_count - 1)

    cross.wait_send()
    for i in range(half_groups):
        int_copy(y * half_groups + i).wait_send()
    for zz in range(z_count):
        for h in range(2):

            @pl.when(has_r & (zz <= z))
            def _():
                copy(RIGHT, zz, x, h).wait_send()

            @pl.when(has_l & (zz >= z))
            def _():
                copy(LEFT, zz, x, h).wait_send()

            copy(ACROSS, zz, x, h).wait_send()
            copy(CORE, zz, x, h).wait_send()
            copy(CORE2, zz, 1 - x, h).wait_send()

    @pl.loop(0, occ_here // step)
    def _(i):
        cols = pl.ds(pl.multiple_of(i * step, step), step)
        pltpu.make_async_copy(out_scr.at[cols, :], out_hbm.at[cols, :], out_sem.at[i]).wait()


def relayed(amplitudes, amp_mask, integrals, int_mask, owner, occ_energy, vir_energy):
    z_count = lax.axis_size("wide") // 4
    k_total = amplitudes.shape[0] * lax.axis_size("wide") * 2
    occ_here, vir_here = occ_energy.shape[0], integrals.shape[1]
    vmem = pl.BlockSpec(memory_space=pltpu.VMEM)
    smem = pl.BlockSpec(memory_space=pltpu.SMEM)
    anywhere = pl.BlockSpec(memory_space=pl.ANY)
    dma = pltpu.SemaphoreType.DMA
    return pl.pallas_call(
        functools.partial(ladder_kernel, z_count),
        out_shape=jax.ShapeDtypeStruct((occ_here, vir_here), jnp.bfloat16),
        in_specs=[anywhere, anywhere, vmem, vmem, smem, vmem, vmem],
        out_specs=anywhere,
        scratch_shapes=[
            pltpu.VMEM((k_total, occ_here), jnp.bfloat16),
            pltpu.VMEM((k_total, vir_here), jnp.bfloat16),
            pltpu.VMEM((occ_here, vir_here), jnp.float32),
            pltpu.VMEM((occ_here, vir_here), jnp.float32),
            pltpu.VMEM((k_total // TILE, occ_here), jnp.float32),
            pltpu.VMEM((k_total // TILE, vir_here), jnp.float32),
            pltpu.VMEM((occ_here, vir_here), jnp.bfloat16),
            pltpu.VMEM((occ_here, LANES), jnp.float32),
            dma((2,)),
            dma,
            dma((z_count,)),
            dma((z_count,)),
            dma((5, 2 * z_count)),
            dma((8 * z_count,)),
            dma((occ_here // 256,)),
        ],
        compiler_params=pltpu.CompilerParams(
            collective_id=0, has_side_effects=True, vmem_limit_bytes=40 * 2**20
        ),
        cost_estimate=pl.CostEstimate(
            flops=2 * k_total * occ_here * vir_here, bytes_accessed=4 * 2**20, transcendentals=0
        ),
    )(
        amplitudes,
        integrals,
        amp_mask,
        int_mask,
        owner,
        occ_energy.reshape(-1, LANES),
        vir_energy.reshape(-1, LANES),
    )


def fits(mesh, amplitudes, integrals):
    wide, narrow = mesh.shape["wide"], mesh.shape["narrow"]
    return (
        narrow == 2
        and wide % 8 == 0
        and amplitudes.shape[0] == wide * narrow * TILE
        and amplitudes.shape[1] % (2 * 1024) == 0
        and (integrals.shape[1] // wide) % LANES == 0
    )


def solution(mesh):
    def run(amplitudes, amp_mask, integrals, int_mask, owner, occ_energy, vir_energy):
        body = relayed if fits(mesh, amplitudes, integrals) else shards
        return jax.shard_map(
            body,
            mesh=mesh,
            in_specs=(
                P(("wide", "narrow"), None),
                P(),
                P("narrow", "wide"),
                P(),
                P(),
                P("narrow"),
                P(),
            ),
            out_specs=P("narrow", "wide"),
            check_vma=False,
        )(amplitudes, amp_mask, integrals, int_mask, owner, occ_energy, vir_energy)

    return run
```

```python
import functools

import jax
import jax.numpy as jnp
from jax import lax
from jax.experimental import pallas as pl
from jax.experimental.pallas import tpu as pltpu
from jax.sharding import PartitionSpec as P

TILE = 64


def contract_rows(summed, rows_in, int_part):
    return summed + lax.dot_general(
        rows_in, int_part, (((0,), (0,)), ((), ())), preferred_element_type=jnp.float32
    )


def contract_all(amp_full, int_full, starting):
    k_total = amp_full.shape[0]
    block_rows = min(512, k_total)
    summed = starting
    for first_row in range(0, k_total, block_rows):
        summed = contract_rows(
            summed,
            amp_full[first_row : first_row + block_rows],
            int_full[first_row : first_row + block_rows],
        )
    return summed


def shards(amplitudes, amp_mask, integrals, int_mask, owner, occ_energy, vir_energy):
    tile_width = TILE
    narrow_count = lax.axis_size("narrow")
    wide_index = lax.axis_index("wide")
    narrow_index = lax.axis_index("narrow")
    src_rows = amplitudes.shape[0]
    occ_all = amplitudes.shape[1]
    occ_here = occ_energy.shape[0]
    vir_here = integrals.shape[1]
    first_src = (wide_index * narrow_count + narrow_index) * src_rows
    src_tiles = (first_src + jnp.arange(src_rows, dtype=jnp.int32)) // tile_width
    src_mask = jnp.take(amp_mask, src_tiles, axis=0)
    src_wide = jnp.broadcast_to(
        src_mask[:, :, None], (src_rows, occ_all // tile_width, tile_width)
    ).reshape(src_rows, occ_all)
    masked = jnp.where(src_wide == 1, amplitudes, jnp.zeros((), amplitudes.dtype))
    vir_tiles_here = vir_here // tile_width
    slot_ids = wide_index * vir_tiles_here + jnp.arange(vir_tiles_here, dtype=jnp.int32)
    tile_ids = jnp.take(owner, slot_ids)
    vir_mask = jnp.take(int_mask, tile_ids, axis=1)
    int_rows = integrals.shape[0]
    row_tiles = int_rows // tile_width
    local_mask = lax.dynamic_slice_in_dim(vir_mask, narrow_index * row_tiles, row_tiles, 0)
    local_wide = jnp.broadcast_to(
        local_mask[:, None, :, None], (row_tiles, tile_width, vir_tiles_here, tile_width)
    ).reshape(int_rows, vir_here)
    int_masked = jnp.where(local_wide == 1, integrals, jnp.zeros((), integrals.dtype))
    int_full = lax.all_gather(int_masked, "narrow", axis=0, tiled=True)
    starting = jnp.zeros((occ_here, vir_here), jnp.float32)
    regrouped = lax.all_to_all(masked, "narrow", split_axis=1, concat_axis=0, tiled=True)
    amp_full = lax.all_gather(regrouped, "wide", axis=0, tiled=True)
    ladder = contract_all(amp_full, int_full, starting)
    vir_energy_here = jnp.take(vir_energy.reshape(-1, tile_width), tile_ids, axis=0).reshape(
        vir_here
    )
    denominator = vir_energy_here[None, :] - occ_energy[:, None]
    return (ladder / denominator).astype(jnp.bfloat16)


MESH = pl.DeviceIdType.MESH
LANES = 128


def lookup(table, z, y):
    value = jnp.int32(table[0][0])
    for zz in range(len(table)):
        for yy in range(2):
            if table[zz][yy] != table[0][0]:
                value = jnp.where((z == zz) & (y == yy), jnp.int32(table[zz][yy]), value)
    return value


ARRIVALS = (
    ("z", 0, 1, 3.5),
    ("x", 0, 0, 3.5),
    ("y", 1, 0, 5.5),
    ("z", 0, 2, 6.5),
    ("x", 0, 1, 6.5),
    ("z", 1, 1, 9.0),
    ("x", 1, 0, 9.0),
    ("z", 0, 3, 10.0),
    ("z", 1, 2, 12.0),
    ("x", 0, 2, 13.0),
    ("x", 1, 1, 14.5),
    ("z", 1, 3, 16.0),
    ("x", 0, 3, 17.0),
    ("x", 1, 2, 20.0),
    ("x", 1, 3, 23.0),
)


def schedule(z_count):
    half = z_count // 2
    event = {(kind, dist): i for i, (kind, cross, dist, _) in enumerate(ARRIVALS) if cross == 1}
    event["z", 0] = event["y", 0]
    chunks = [[None] * 2 for _ in range(z_count)]
    units = [[None] * 2 for _ in range(z_count)]
    place = [0] * (2 * z_count)
    for z in range(z_count):
        for y in range(2):
            groups = sorted(range(y * half, (y + 1) * half), key=lambda g: abs(g - z))
            chunks[z][y] = [(g, e) for g in groups for e in range(2)]
        for y in range(2):
            remote = chunks[z][1 - y]
            rows = []
            for g in range(z_count):
                for e in range(2):
                    at = event["xz"[1 - e], abs(g - z)]
                    n = remote.index((g, e)) if (g, e) in remote else -1
                    ready = max(ARRIVALS[at][3], 8.0 + 5.2 * n)
                    rows.append((ready, at, g, e, n))
            rows.sort()
            units[z][y] = rows
            for i, (ready, at, _, _, _) in enumerate(rows):
                late = [j for j, a in enumerate(ARRIVALS) if a[3] + 1.0 >= ready]
                place[i] = max(place[i], at, late[0] if late else len(ARRIVALS) - 1)
    for i in range(1, len(place)):
        place[i] = max(place[i], place[i - 1])
    return chunks, units, place


def ladder_kernel(
    z_count,
    amp_hbm,
    int_hbm,
    amask_hbm,
    imask_hbm,
    owner_hbm,
    occ_hbm,
    vir_hbm,
    out_ref,
    amp_scr,
    int_scr,
    acc,
    recip,
    amask,
    imask,
    occ_cols,
    amask_ref,
    imask_ref,
    owner_ref,
    occ_ref,
    vir_ref,
    own_sem,
    ycross_send,
    int_send,
    int_recv,
    send_sem,
    recv_sem,
):
    w = lax.axis_index("wide")
    y = lax.axis_index("narrow")
    z, x, c = w // 4, (w // 2) % 2, w % 2
    rows = amp_hbm.shape[0]
    occ_here, vir_here = acc.shape
    unit = int_scr.shape[0] // (2 * z_count)
    half_groups = z_count // 2
    chunks, units, place = schedule(z_count)

    def wide_id(zz, xx, cc):
        return zz * 4 + xx * 2 + cc

    y_peer = (w, 1 - y)
    x_peer = (wide_id(z, 1 - x, c), y)
    c_peer = (wide_id(z, x, 1 - c), y)
    r_peer = (w + 4, y)
    l_peer = (w - 4, y)
    has_r, has_l = z < z_count - 1, z > 0

    barrier = pltpu.get_barrier_semaphore()
    for peer in (y_peer, x_peer, c_peer):
        pl.semaphore_signal(barrier, inc=1, device_id=peer, device_id_type=MESH)

    @pl.when(has_r)
    def _():
        pl.semaphore_signal(barrier, inc=1, device_id=r_peer, device_id_type=MESH)

    @pl.when(has_l)
    def _():
        pl.semaphore_signal(barrier, inc=1, device_id=l_peer, device_id_type=MESH)

    small = [
        pltpu.make_async_copy(src, dst, own_sem.at[2 + i])
        for i, (src, dst) in enumerate(
            (
                (amask_hbm, amask_ref),
                (imask_hbm, imask_ref),
                (owner_hbm, owner_ref),
                (occ_hbm, occ_ref),
                (vir_hbm, vir_ref),
            )
        )
    ]
    for one in small:
        one.start()

    pl.semaphore_wait(barrier, 3 + jnp.where(has_r, 1, 0) + jnp.where(has_l, 1, 0))

    def block_id(zz, xx, cc, h):
        return wide_id(zz, xx, cc) * 2 + h

    def block(zz, xx, cc, h):
        first = pl.multiple_of(block_id(zz, xx, cc, h) * rows, rows)
        return amp_scr.at[pl.ds(first, rows), :]

    def half_cols(yy):
        return amp_hbm.at[:, pl.ds(pl.multiple_of(yy * occ_here, LANES), occ_here)]

    RIGHT, LEFT, ACROSS, CORE, CORE2 = range(5)
    peers = (r_peer, l_peer, x_peer, c_peer, c_peer)

    def copy(kind, zz, xx, h, src=None):
        there = block(zz, xx, c, h)
        return pltpu.make_async_remote_copy(
            src_ref=there if src is None else src,
            dst_ref=there,
            send_sem=send_sem.at[kind, zz * 2 + h],
            recv_sem=recv_sem.at[block_id(zz, xx, c, h)],
            device_id=peers[kind],
            device_id_type=MESH,
        )

    def arrived(zz, xx, cc, h):
        here = block(zz, xx, cc, h)
        pltpu.make_async_remote_copy(
            src_ref=here,
            dst_ref=here,
            send_sem=send_sem.at[CORE, zz * 2 + h],
            recv_sem=recv_sem.at[block_id(zz, xx, cc, h)],
            device_id=c_peer,
            device_id_type=MESH,
        ).wait_recv()

    cross = pltpu.make_async_remote_copy(
        src_ref=half_cols(1 - y),
        dst_ref=block(z, x, c, y),
        send_sem=ycross_send,
        recv_sem=recv_sem.at[block_id(z, x, c, y)],
        device_id=y_peer,
        device_id_type=MESH,
    )
    cross.start()

    def spread_own(h, src):
        @pl.when(has_r)
        def _():
            copy(RIGHT, z, x, h, src).start()

        @pl.when(has_l)
        def _():
            copy(LEFT, z, x, h, src).start()

        copy(ACROSS, z, x, h, src).start()
        copy(CORE, z, x, h, src).start()

    spread_own(y, half_cols(y))

    def unit_row(g, far):
        return (g * 2 + x + far - 2 * x * far) * unit

    def int_chunk(n):
        g = lookup([[r[n][0] for r in row] for row in chunks], z, y)
        first = unit_row(g, chunks[0][0][n][1])
        return pltpu.make_async_remote_copy(
            src_ref=int_hbm.at[
                pl.ds(pl.multiple_of(first - y * half_groups * 2 * unit, unit), unit), :
            ],
            dst_ref=int_scr.at[pl.ds(pl.multiple_of(first, unit), unit), :],
            send_sem=int_send.at[n],
            recv_sem=int_recv.at[n],
            device_id=y_peer,
            device_id_type=MESH,
        )

    n_chunks = 2 * half_groups
    int_chunk(0).start()

    own_copy = pltpu.make_async_copy(half_cols(y), block(z, x, c, y), own_sem.at[0])
    own_copy.start()
    kept = half_groups * 2 * unit
    held = pltpu.make_async_copy(
        int_hbm, int_scr.at[pl.ds(pl.multiple_of(y * kept, unit), kept), :], own_sem.at[1]
    )
    held.start()

    slots = vir_here // TILE

    def prepare_masks():
        for one in small:
            one.wait()
        lane = lax.broadcasted_iota(jnp.int32, (1, vir_here), 1) // TILE
        tile_of = jnp.zeros((1, vir_here), jnp.int32)
        for j in range(slots):
            tile_of = jnp.where(lane == j, owner_ref[w * slots + j], tile_of)
        q_tiles = imask_ref.shape[1]
        pick = lax.broadcasted_iota(jnp.int32, (q_tiles, vir_here), 0) == tile_of
        imask[...] = jnp.dot(
            imask_ref[...].astype(jnp.float32).astype(jnp.bfloat16),
            jnp.where(pick, 1.0, 0.0).astype(jnp.bfloat16),
            preferred_element_type=jnp.float32,
        )
        p_tiles = amask_ref.shape[1]
        p_lane = lax.broadcasted_iota(jnp.int32, (p_tiles, occ_here), 1) // TILE
        p_tile = y * (occ_here // TILE) + p_lane
        pick_p = lax.broadcasted_iota(jnp.int32, (p_tiles, occ_here), 0) == p_tile
        amask[...] = jnp.dot(
            amask_ref[...].astype(jnp.float32).astype(jnp.bfloat16),
            jnp.where(pick_p, 1.0, 0.0).astype(jnp.bfloat16),
            preferred_element_type=jnp.float32,
        )

    low = lax.broadcasted_iota(jnp.int32, (1, LANES), 1) < TILE

    def energies(tile, upper):
        row = vir_ref[pl.ds(tile // 2, 1), :]
        turned = jnp.concatenate([row[:, TILE:], row[:, :TILE]], axis=1)
        odd = jnp.full((1, LANES), tile % 2, jnp.int32) == upper
        return jnp.where(odd, row, turned)

    def prepare_reciprocals():
        occ_t = jnp.transpose(occ_ref[...])
        for j in range(occ_here // LANES):
            occ_cols[j * LANES : (j + 1) * LANES, :] = jnp.broadcast_to(
                occ_t[:, j : j + 1], (LANES, LANES)
            )
        for j in range(slots // 2):
            first = energies(owner_ref[w * slots + 2 * j], 0)
            second = energies(owner_ref[w * slots + 2 * j + 1], 1)
            vir_row = jnp.where(low, first, second)

            @pl.loop(0, occ_here // LANES)
            def _(i):
                at = pl.ds(pl.multiple_of(i * LANES, LANES), LANES)
                recip[at, j * LANES : (j + 1) * LANES] = 1.0 / (vir_row - occ_cols[at, :])

    step = 256

    def multiply(i):
        g = lookup([[r[i][2] for r in row] for row in units], z, y)
        far = lookup([[r[i][3] for r in row] for row in units], z, y)
        first_row = unit_row(g, far)
        xx = x + far - 2 * x * far
        for h in range(2):
            arrived(g, xx, 1 - c, h)

        order = [[r[i][4] for r in row] for row in units]
        here = int_scr.at[pl.ds(pl.multiple_of(first_row, unit), unit), :]
        for n in range(n_chunks):
            if any(n in row for row in order):

                @pl.when(lookup(order, z, y) == n)
                def _():
                    pltpu.make_async_remote_copy(
                        src_ref=here,
                        dst_ref=here,
                        send_sem=int_send.at[n],
                        recv_sem=int_recv.at[n],
                        device_id=y_peer,
                        device_id_type=MESH,
                    ).wait_recv()

        tiles = unit // TILE
        for t in range(tiles):
            at = pl.ds(pl.multiple_of(first_row + t * TILE, TILE), TILE)
            row = imask[pl.ds(first_row // TILE + t, 1), :].astype(jnp.bfloat16)
            int_scr[at, :] = int_scr[at, :] * jnp.broadcast_to(row, (TILE, vir_here))

        @pl.loop(0, occ_here // step)
        def _(p):
            cols = pl.ds(pl.multiple_of(p * step, step), step)
            parts = []
            for t in range(tiles):
                at = pl.ds(pl.multiple_of(first_row + t * TILE, TILE), TILE)
                row = amask[pl.ds(first_row // TILE + t, 1), cols].astype(jnp.bfloat16)
                parts.append(amp_scr[at, cols] * jnp.broadcast_to(row, (TILE, step)))
            left = jnp.concatenate(parts, axis=0)
            term = lax.dot_general(
                left,
                int_scr[pl.ds(pl.multiple_of(first_row, unit), unit), :],
                (((0,), (0,)), ((), ())),
                preferred_element_type=jnp.float32,
            )
            if i == 0:
                acc[cols, :] = term
            elif i < 2 * z_count - 1:
                acc[cols, :] += term
            else:
                out_ref[cols, :] = ((acc[cols, :] + term) * recip[cols, :]).astype(jnp.bfloat16)

    def each_side(dist, act):
        if dist == 0:
            act(z, None)
            return

        @pl.when(z - dist >= 0)
        def _():
            act(z - dist, RIGHT)

        @pl.when(z + dist <= z_count - 1)
        def _():
            act(z + dist, LEFT)

    def arrival(kind, h, dist):
        def from_z(zz, onward):
            arrived(zz, x, c, h)

            @pl.when(has_r if onward == RIGHT else has_l)
            def _():
                copy(onward, zz, x, h).start()

            copy(ACROSS, zz, x, h).start()
            copy(CORE, zz, x, h).start()

        def from_x(zz, _):
            arrived(zz, 1 - x, c, h)
            copy(CORE2, zz, 1 - x, h).start()

        if kind == "y":
            arrived(z, x, c, h)
            spread_own(h, block(z, x, c, h))
        else:
            each_side(dist, from_z if kind == "z" else from_x)

    sent = 1
    for at, (kind, crossed, dist, when) in enumerate(ARRIVALS):
        arrival(kind, 1 - y if crossed else y, dist)
        if at == 0:
            prepare_masks()
        if kind == "y":
            prepare_reciprocals()
        while sent < n_chunks and when >= 5.2 * (sent - 1) + 4.0:
            if sent >= 2:
                int_chunk(sent - 2).wait_send()
            int_chunk(sent).start()
            sent += 1
        for i in range(2 * z_count):
            if place[i] == at:
                if i == 0:
                    own_copy.wait()
                    held.wait()
                multiply(i)

    cross.wait_send()
    for n in range(n_chunks - 2, n_chunks):
        int_chunk(n).wait_send()
    for zz in range(z_count):
        for h in range(2):

            @pl.when(has_r & (zz <= z))
            def _():
                copy(RIGHT, zz, x, h).wait_send()

            @pl.when(has_l & (zz >= z))
            def _():
                copy(LEFT, zz, x, h).wait_send()

            copy(ACROSS, zz, x, h).wait_send()
            copy(CORE, zz, x, h).wait_send()
            copy(CORE2, zz, 1 - x, h).wait_send()


def relayed(amplitudes, amp_mask, integrals, int_mask, owner, occ_energy, vir_energy):
    z_count = lax.axis_size("wide") // 4
    k_total = amplitudes.shape[0] * lax.axis_size("wide") * 2
    occ_here, vir_here = occ_energy.shape[0], integrals.shape[1]
    hbm = pl.BlockSpec(memory_space=pltpu.HBM)
    dma = pltpu.SemaphoreType.DMA
    occ_rows, vir_rows = occ_here // LANES, vir_energy.shape[0] // LANES
    return pl.pallas_call(
        functools.partial(ladder_kernel, z_count),
        out_shape=jax.ShapeDtypeStruct((occ_here, vir_here), jnp.bfloat16),
        in_specs=[hbm] * 7,
        out_specs=pl.BlockSpec(memory_space=pltpu.VMEM),
        scratch_shapes=[
            pltpu.VMEM((k_total, occ_here), jnp.bfloat16),
            pltpu.VMEM((k_total, vir_here), jnp.bfloat16),
            pltpu.VMEM((occ_here, vir_here), jnp.float32),
            pltpu.VMEM((occ_here, vir_here), jnp.float32),
            pltpu.VMEM((k_total // TILE, occ_here), jnp.float32),
            pltpu.VMEM((k_total // TILE, vir_here), jnp.float32),
            pltpu.VMEM((occ_here, LANES), jnp.float32),
            pltpu.VMEM(amp_mask.shape, jnp.int32),
            pltpu.VMEM(int_mask.shape, jnp.int32),
            pltpu.SMEM(owner.shape, jnp.int32),
            pltpu.VMEM((occ_rows, LANES), jnp.float32),
            pltpu.VMEM((vir_rows, LANES), jnp.float32),
            dma((7,)),
            dma,
            dma((z_count,)),
            dma((z_count,)),
            dma((5, 2 * z_count)),
            dma((8 * z_count,)),
        ],
        compiler_params=pltpu.CompilerParams(
            collective_id=0, has_side_effects=True, vmem_limit_bytes=40 * 2**20
        ),
        cost_estimate=pl.CostEstimate(
            flops=2 * k_total * occ_here * vir_here, bytes_accessed=4 * 2**20, transcendentals=0
        ),
    )(
        amplitudes,
        integrals,
        amp_mask,
        int_mask,
        owner,
        occ_energy.reshape(-1, LANES),
        vir_energy.reshape(-1, LANES),
    )


def fits(mesh, amplitudes, integrals):
    wide, narrow = mesh.shape["wide"], mesh.shape["narrow"]
    return (
        narrow == 2
        and wide == 16
        and amplitudes.shape[0] == wide * narrow * TILE
        and amplitudes.shape[1] % (2 * 1024) == 0
        and (integrals.shape[1] // wide) % LANES == 0
    )


def solution(mesh):
    def run(amplitudes, amp_mask, integrals, int_mask, owner, occ_energy, vir_energy):
        body = relayed if fits(mesh, amplitudes, integrals) else shards
        return jax.shard_map(
            body,
            mesh=mesh,
            in_specs=(
                P(("wide", "narrow"), None),
                P(),
                P("narrow", "wide"),
                P(),
                P(),
                P("narrow"),
                P(),
            ),
            out_specs=P("narrow", "wide"),
            check_vma=False,
        )(amplitudes, amp_mask, integrals, int_mask, owner, occ_energy, vir_energy)

    return run
```

```python
import functools

import jax
import jax.numpy as jnp
from jax import lax
from jax.experimental import pallas as pl
from jax.experimental.pallas import tpu as pltpu
from jax.sharding import PartitionSpec as P

TILE = 64


def contract_rows(summed, rows_in, int_part):
    return summed + lax.dot_general(
        rows_in, int_part, (((0,), (0,)), ((), ())), preferred_element_type=jnp.float32
    )


def contract_all(amp_full, int_full, starting):
    k_total = amp_full.shape[0]
    block_rows = min(512, k_total)
    summed = starting
    for first_row in range(0, k_total, block_rows):
        summed = contract_rows(
            summed,
            amp_full[first_row : first_row + block_rows],
            int_full[first_row : first_row + block_rows],
        )
    return summed


def shards(amplitudes, amp_mask, integrals, int_mask, owner, occ_energy, vir_energy):
    tile_width = TILE
    narrow_count = lax.axis_size("narrow")
    wide_index = lax.axis_index("wide")
    narrow_index = lax.axis_index("narrow")
    src_rows = amplitudes.shape[0]
    occ_all = amplitudes.shape[1]
    occ_here = occ_energy.shape[0]
    vir_here = integrals.shape[1]
    first_src = (wide_index * narrow_count + narrow_index) * src_rows
    src_tiles = (first_src + jnp.arange(src_rows, dtype=jnp.int32)) // tile_width
    src_mask = jnp.take(amp_mask, src_tiles, axis=0)
    src_wide = jnp.broadcast_to(
        src_mask[:, :, None], (src_rows, occ_all // tile_width, tile_width)
    ).reshape(src_rows, occ_all)
    masked = jnp.where(src_wide == 1, amplitudes, jnp.zeros((), amplitudes.dtype))
    vir_tiles_here = vir_here // tile_width
    slot_ids = wide_index * vir_tiles_here + jnp.arange(vir_tiles_here, dtype=jnp.int32)
    tile_ids = jnp.take(owner, slot_ids)
    vir_mask = jnp.take(int_mask, tile_ids, axis=1)
    int_rows = integrals.shape[0]
    row_tiles = int_rows // tile_width
    local_mask = lax.dynamic_slice_in_dim(vir_mask, narrow_index * row_tiles, row_tiles, 0)
    local_wide = jnp.broadcast_to(
        local_mask[:, None, :, None], (row_tiles, tile_width, vir_tiles_here, tile_width)
    ).reshape(int_rows, vir_here)
    int_masked = jnp.where(local_wide == 1, integrals, jnp.zeros((), integrals.dtype))
    int_full = lax.all_gather(int_masked, "narrow", axis=0, tiled=True)
    starting = jnp.zeros((occ_here, vir_here), jnp.float32)
    regrouped = lax.all_to_all(masked, "narrow", split_axis=1, concat_axis=0, tiled=True)
    amp_full = lax.all_gather(regrouped, "wide", axis=0, tiled=True)
    ladder = contract_all(amp_full, int_full, starting)
    vir_energy_here = jnp.take(vir_energy.reshape(-1, tile_width), tile_ids, axis=0).reshape(
        vir_here
    )
    denominator = vir_energy_here[None, :] - occ_energy[:, None]
    return (ladder / denominator).astype(jnp.bfloat16)


MESH = pl.DeviceIdType.MESH
LANES = 128


def lookup(table, z, y):
    value = jnp.int32(table[0][0])
    for zz in range(len(table)):
        for yy in range(2):
            if table[zz][yy] != table[0][0]:
                value = jnp.where((z == zz) & (y == yy), jnp.int32(table[zz][yy]), value)
    return value


ARRIVALS = (
    ("z", 0, 1, 3.5),
    ("x", 0, 0, 3.5),
    ("y", 1, 0, 5.5),
    ("z", 0, 2, 6.5),
    ("x", 0, 1, 6.5),
    ("z", 1, 1, 9.0),
    ("x", 1, 0, 9.0),
    ("z", 0, 3, 10.0),
    ("z", 1, 2, 12.0),
    ("x", 0, 2, 13.0),
    ("x", 1, 1, 14.5),
    ("z", 1, 3, 16.0),
    ("x", 0, 3, 17.0),
    ("x", 1, 2, 20.0),
    ("x", 1, 3, 23.0),
)


def schedule(z_count):
    half = z_count // 2
    event = {(kind, dist): i for i, (kind, cross, dist, _) in enumerate(ARRIVALS) if cross == 1}
    event["z", 0] = event["y", 0]
    chunks = [[None] * 2 for _ in range(z_count)]
    units = [[None] * 2 for _ in range(z_count)]
    place = [0] * (2 * z_count)
    for z in range(z_count):
        for y in range(2):
            groups = sorted(range(y * half, (y + 1) * half), key=lambda g: abs(g - z))
            chunks[z][y] = [(g, e) for g in groups for e in range(2)]
        for y in range(2):
            remote = chunks[z][1 - y]
            rows = []
            for g in range(z_count):
                for e in range(2):
                    at = event["xz"[1 - e], abs(g - z)]
                    n = remote.index((g, e)) if (g, e) in remote else -1
                    ready = max(ARRIVALS[at][3], 8.0 + 5.2 * n)
                    rows.append((ready, at, g, e, n))
            rows.sort()
            units[z][y] = rows
            for i, (ready, at, _, _, _) in enumerate(rows):
                late = [j for j, a in enumerate(ARRIVALS) if a[3] + 1.0 >= ready]
                place[i] = max(place[i], at, late[0] if late else len(ARRIVALS) - 1)
    for i in range(1, len(place)):
        place[i] = max(place[i], place[i - 1])
    return chunks, units, place


def ladder_kernel(
    z_count,
    amp_hbm,
    int_hbm,
    amask_hbm,
    imask_hbm,
    owner_hbm,
    occ_hbm,
    vir_hbm,
    out_hbm,
    amp_scr,
    int_scr,
    acc,
    recip,
    amask,
    imask,
    occ_cols,
    amask_ref,
    imask_ref,
    owner_ref,
    occ_ref,
    vir_ref,
    out_scr,
    out_sem,
    own_sem,
    ycross_send,
    int_send,
    int_recv,
    send_sem,
    recv_sem,
):
    w = lax.axis_index("wide")
    y = lax.axis_index("narrow")
    z, x, c = w // 4, (w // 2) % 2, w % 2
    rows = amp_hbm.shape[0]
    occ_here, vir_here = acc.shape
    unit = int_scr.shape[0] // (2 * z_count)
    half_groups = z_count // 2
    chunks, units, place = schedule(z_count)

    def wide_id(zz, xx, cc):
        return zz * 4 + xx * 2 + cc

    y_peer = (w, 1 - y)
    x_peer = (wide_id(z, 1 - x, c), y)
    c_peer = (wide_id(z, x, 1 - c), y)
    r_peer = (w + 4, y)
    l_peer = (w - 4, y)
    has_r, has_l = z < z_count - 1, z > 0

    barrier = pltpu.get_barrier_semaphore()
    for peer in (y_peer, x_peer, c_peer):
        pl.semaphore_signal(barrier, inc=1, device_id=peer, device_id_type=MESH)

    @pl.when(has_r)
    def _():
        pl.semaphore_signal(barrier, inc=1, device_id=r_peer, device_id_type=MESH)

    @pl.when(has_l)
    def _():
        pl.semaphore_signal(barrier, inc=1, device_id=l_peer, device_id_type=MESH)

    small = [
        pltpu.make_async_copy(src, dst, own_sem.at[2 + i])
        for i, (src, dst) in enumerate(
            (
                (amask_hbm, amask_ref),
                (imask_hbm, imask_ref),
                (owner_hbm, owner_ref),
                (occ_hbm, occ_ref),
                (vir_hbm, vir_ref),
            )
        )
    ]
    for one in small:
        one.start()

    pl.semaphore_wait(barrier, 3 + jnp.where(has_r, 1, 0) + jnp.where(has_l, 1, 0))

    def block_id(zz, xx, cc, h):
        return wide_id(zz, xx, cc) * 2 + h

    def block(zz, xx, cc, h):
        first = pl.multiple_of(block_id(zz, xx, cc, h) * rows, rows)
        return amp_scr.at[pl.ds(first, rows), :]

    def half_cols(yy):
        return amp_hbm.at[:, pl.ds(pl.multiple_of(yy * occ_here, LANES), occ_here)]

    RIGHT, LEFT, ACROSS, CORE, CORE2 = range(5)
    peers = (r_peer, l_peer, x_peer, c_peer, c_peer)

    def copy(kind, zz, xx, h, src=None):
        there = block(zz, xx, c, h)
        return pltpu.make_async_remote_copy(
            src_ref=there if src is None else src,
            dst_ref=there,
            send_sem=send_sem.at[kind, zz * 2 + h],
            recv_sem=recv_sem.at[block_id(zz, xx, c, h)],
            device_id=peers[kind],
            device_id_type=MESH,
        )

    def arrived(zz, xx, cc, h):
        here = block(zz, xx, cc, h)
        pltpu.make_async_remote_copy(
            src_ref=here,
            dst_ref=here,
            send_sem=send_sem.at[CORE, zz * 2 + h],
            recv_sem=recv_sem.at[block_id(zz, xx, cc, h)],
            device_id=c_peer,
            device_id_type=MESH,
        ).wait_recv()

    cross = pltpu.make_async_remote_copy(
        src_ref=half_cols(1 - y),
        dst_ref=block(z, x, c, y),
        send_sem=ycross_send,
        recv_sem=recv_sem.at[block_id(z, x, c, y)],
        device_id=y_peer,
        device_id_type=MESH,
    )
    cross.start()

    def spread_own(h, src):
        @pl.when(has_r)
        def _():
            copy(RIGHT, z, x, h, src).start()

        @pl.when(has_l)
        def _():
            copy(LEFT, z, x, h, src).start()

        copy(ACROSS, z, x, h, src).start()
        copy(CORE, z, x, h, src).start()

    spread_own(y, half_cols(y))

    def unit_row(g, far):
        return (g * 2 + x + far - 2 * x * far) * unit

    def int_chunk(n):
        g = lookup([[r[n][0] for r in row] for row in chunks], z, y)
        first = unit_row(g, chunks[0][0][n][1])
        return pltpu.make_async_remote_copy(
            src_ref=int_hbm.at[
                pl.ds(pl.multiple_of(first - y * half_groups * 2 * unit, unit), unit), :
            ],
            dst_ref=int_scr.at[pl.ds(pl.multiple_of(first, unit), unit), :],
            send_sem=int_send.at[n],
            recv_sem=int_recv.at[n],
            device_id=y_peer,
            device_id_type=MESH,
        )

    n_chunks = 2 * half_groups
    int_chunk(0).start()

    own_copy = pltpu.make_async_copy(half_cols(y), block(z, x, c, y), own_sem.at[0])
    own_copy.start()
    kept = half_groups * 2 * unit
    held = pltpu.make_async_copy(
        int_hbm, int_scr.at[pl.ds(pl.multiple_of(y * kept, unit), kept), :], own_sem.at[1]
    )
    held.start()

    slots = vir_here // TILE

    def prepare_masks():
        for one in small:
            one.wait()
        lane = lax.broadcasted_iota(jnp.int32, (1, vir_here), 1) // TILE
        tile_of = jnp.zeros((1, vir_here), jnp.int32)
        for j in range(slots):
            tile_of = jnp.where(lane == j, owner_ref[w * slots + j], tile_of)
        q_tiles = imask_ref.shape[1]
        pick = lax.broadcasted_iota(jnp.int32, (q_tiles, vir_here), 0) == tile_of
        imask[...] = jnp.dot(
            imask_ref[...].astype(jnp.float32).astype(jnp.bfloat16),
            jnp.where(pick, 1.0, 0.0).astype(jnp.bfloat16),
            preferred_element_type=jnp.float32,
        )
        p_tiles = amask_ref.shape[1]
        p_lane = lax.broadcasted_iota(jnp.int32, (p_tiles, occ_here), 1) // TILE
        p_tile = y * (occ_here // TILE) + p_lane
        pick_p = lax.broadcasted_iota(jnp.int32, (p_tiles, occ_here), 0) == p_tile
        amask[...] = jnp.dot(
            amask_ref[...].astype(jnp.float32).astype(jnp.bfloat16),
            jnp.where(pick_p, 1.0, 0.0).astype(jnp.bfloat16),
            preferred_element_type=jnp.float32,
        )

    low = lax.broadcasted_iota(jnp.int32, (1, LANES), 1) < TILE

    def energies(tile, upper):
        row = vir_ref[pl.ds(tile // 2, 1), :]
        turned = jnp.concatenate([row[:, TILE:], row[:, :TILE]], axis=1)
        odd = jnp.full((1, LANES), tile % 2, jnp.int32) == upper
        return jnp.where(odd, row, turned)

    def prepare_reciprocals():
        occ_t = jnp.transpose(occ_ref[...])
        for j in range(occ_here // LANES):
            occ_cols[j * LANES : (j + 1) * LANES, :] = jnp.broadcast_to(
                occ_t[:, j : j + 1], (LANES, LANES)
            )
        for j in range(slots // 2):
            first = energies(owner_ref[w * slots + 2 * j], 0)
            second = energies(owner_ref[w * slots + 2 * j + 1], 1)
            vir_row = jnp.where(low, first, second)

            @pl.loop(0, occ_here // LANES)
            def _(i):
                at = pl.ds(pl.multiple_of(i * LANES, LANES), LANES)
                recip[at, j * LANES : (j + 1) * LANES] = 1.0 / (vir_row - occ_cols[at, :])

    step = 256

    def out_copy(p):
        cols = pl.ds(pl.multiple_of(p * step, step), step)
        return pltpu.make_async_copy(out_scr.at[cols, :], out_hbm.at[cols, :], out_sem.at[p])

    def multiply(i):
        g = lookup([[r[i][2] for r in row] for row in units], z, y)
        far = lookup([[r[i][3] for r in row] for row in units], z, y)
        first_row = unit_row(g, far)
        xx = x + far - 2 * x * far
        for h in range(2):
            arrived(g, xx, 1 - c, h)

        order = [[r[i][4] for r in row] for row in units]
        here = int_scr.at[pl.ds(pl.multiple_of(first_row, unit), unit), :]
        for n in range(n_chunks):
            if any(n in row for row in order):

                @pl.when(lookup(order, z, y) == n)
                def _():
                    pltpu.make_async_remote_copy(
                        src_ref=here,
                        dst_ref=here,
                        send_sem=int_send.at[n],
                        recv_sem=int_recv.at[n],
                        device_id=y_peer,
                        device_id_type=MESH,
                    ).wait_recv()

        tiles = unit // TILE
        for t in range(tiles):
            at = pl.ds(pl.multiple_of(first_row + t * TILE, TILE), TILE)
            row = imask[pl.ds(first_row // TILE + t, 1), :].astype(jnp.bfloat16)
            int_scr[at, :] = int_scr[at, :] * jnp.broadcast_to(row, (TILE, vir_here))

        @pl.loop(0, occ_here // step)
        def _(p):
            cols = pl.ds(pl.multiple_of(p * step, step), step)
            parts = []
            for t in range(tiles):
                at = pl.ds(pl.multiple_of(first_row + t * TILE, TILE), TILE)
                row = amask[pl.ds(first_row // TILE + t, 1), cols].astype(jnp.bfloat16)
                parts.append(amp_scr[at, cols] * jnp.broadcast_to(row, (TILE, step)))
            left = jnp.concatenate(parts, axis=0)
            term = lax.dot_general(
                left,
                int_scr[pl.ds(pl.multiple_of(first_row, unit), unit), :],
                (((0,), (0,)), ((), ())),
                preferred_element_type=jnp.float32,
            )
            if i == 0:
                acc[cols, :] = term
            elif i < 2 * z_count - 1:
                acc[cols, :] += term
            else:
                out_scr[cols, :] = ((acc[cols, :] + term) * recip[cols, :]).astype(jnp.bfloat16)
                out_copy(p).start()

    def each_side(dist, act):
        if dist == 0:
            act(z, None)
            return

        @pl.when(z - dist >= 0)
        def _():
            act(z - dist, RIGHT)

        @pl.when(z + dist <= z_count - 1)
        def _():
            act(z + dist, LEFT)

    def arrival(kind, h, dist):
        def from_z(zz, onward):
            arrived(zz, x, c, h)

            @pl.when(has_r if onward == RIGHT else has_l)
            def _():
                copy(onward, zz, x, h).start()

            copy(ACROSS, zz, x, h).start()
            copy(CORE, zz, x, h).start()

        def from_x(zz, _):
            arrived(zz, 1 - x, c, h)
            copy(CORE2, zz, 1 - x, h).start()

        if kind == "y":
            arrived(z, x, c, h)
            spread_own(h, block(z, x, c, h))
        else:
            each_side(dist, from_z if kind == "z" else from_x)

    sent = 1
    for at, (kind, crossed, dist, when) in enumerate(ARRIVALS):
        arrival(kind, 1 - y if crossed else y, dist)
        if at == 0:
            prepare_masks()
        if kind == "y":
            prepare_reciprocals()
        while sent < n_chunks and when >= 5.2 * (sent - 1) + 4.0:
            if sent >= 2:
                int_chunk(sent - 2).wait_send()
            int_chunk(sent).start()
            sent += 1
        for i in range(2 * z_count):
            if place[i] == at:
                if i == 0:
                    own_copy.wait()
                    held.wait()
                multiply(i)

    cross.wait_send()
    for n in range(n_chunks - 2, n_chunks):
        int_chunk(n).wait_send()
    for zz in range(z_count):
        for h in range(2):

            @pl.when(has_r & (zz <= z))
            def _():
                copy(RIGHT, zz, x, h).wait_send()

            @pl.when(has_l & (zz >= z))
            def _():
                copy(LEFT, zz, x, h).wait_send()

            copy(ACROSS, zz, x, h).wait_send()
            copy(CORE, zz, x, h).wait_send()
            copy(CORE2, zz, 1 - x, h).wait_send()

    @pl.loop(0, occ_here // step)
    def _(p):
        out_copy(p).wait()


def relayed(amplitudes, amp_mask, integrals, int_mask, owner, occ_energy, vir_energy):
    z_count = lax.axis_size("wide") // 4
    k_total = amplitudes.shape[0] * lax.axis_size("wide") * 2
    occ_here, vir_here = occ_energy.shape[0], integrals.shape[1]
    hbm = pl.BlockSpec(memory_space=pltpu.HBM)
    dma = pltpu.SemaphoreType.DMA
    occ_rows, vir_rows = occ_here // LANES, vir_energy.shape[0] // LANES
    return pl.pallas_call(
        functools.partial(ladder_kernel, z_count),
        out_shape=jax.ShapeDtypeStruct((occ_here, vir_here), jnp.bfloat16),
        in_specs=[hbm] * 7,
        out_specs=hbm,
        scratch_shapes=[
            pltpu.VMEM((k_total, occ_here), jnp.bfloat16),
            pltpu.VMEM((k_total, vir_here), jnp.bfloat16),
            pltpu.VMEM((occ_here, vir_here), jnp.float32),
            pltpu.VMEM((occ_here, vir_here), jnp.float32),
            pltpu.VMEM((k_total // TILE, occ_here), jnp.float32),
            pltpu.VMEM((k_total // TILE, vir_here), jnp.float32),
            pltpu.VMEM((occ_here, LANES), jnp.float32),
            pltpu.VMEM(amp_mask.shape, jnp.int32),
            pltpu.VMEM(int_mask.shape, jnp.int32),
            pltpu.SMEM(owner.shape, jnp.int32),
            pltpu.VMEM((occ_rows, LANES), jnp.float32),
            pltpu.VMEM((vir_rows, LANES), jnp.float32),
            pltpu.VMEM((occ_here, vir_here), jnp.bfloat16),
            dma((occ_here // 256,)),
            dma((7,)),
            dma,
            dma((z_count,)),
            dma((z_count,)),
            dma((5, 2 * z_count)),
            dma((8 * z_count,)),
        ],
        compiler_params=pltpu.CompilerParams(
            collective_id=0, has_side_effects=True, vmem_limit_bytes=60 * 2**20
        ),
        cost_estimate=pl.CostEstimate(
            flops=2 * k_total * occ_here * vir_here, bytes_accessed=4 * 2**20, transcendentals=0
        ),
    )(
        amplitudes,
        integrals,
        amp_mask,
        int_mask,
        owner,
        occ_energy.reshape(-1, LANES),
        vir_energy.reshape(-1, LANES),
    )


def fits(mesh, amplitudes, integrals):
    wide, narrow = mesh.shape["wide"], mesh.shape["narrow"]
    return (
        narrow == 2
        and wide == 16
        and amplitudes.shape[0] == wide * narrow * TILE
        and amplitudes.shape[1] % (2 * 1024) == 0
        and (integrals.shape[1] // wide) % LANES == 0
    )


def solution(mesh):
    def run(amplitudes, amp_mask, integrals, int_mask, owner, occ_energy, vir_energy):
        body = relayed if fits(mesh, amplitudes, integrals) else shards
        return jax.shard_map(
            body,
            mesh=mesh,
            in_specs=(
                P(("wide", "narrow"), None),
                P(),
                P("narrow", "wide"),
                P(),
                P(),
                P("narrow"),
                P(),
            ),
            out_specs=P("narrow", "wide"),
            check_vma=False,
        )(amplitudes, amp_mask, integrals, int_mask, owner, occ_energy, vir_energy)

    return run
```

```python
import functools

import jax
import jax.numpy as jnp
from jax import lax
from jax.experimental import pallas as pl
from jax.experimental.pallas import tpu as pltpu
from jax.sharding import PartitionSpec as P

TILE = 64


def contract_rows(summed, rows_in, int_part):
    return summed + lax.dot_general(
        rows_in, int_part, (((0,), (0,)), ((), ())), preferred_element_type=jnp.float32
    )


def contract_all(amp_full, int_full, starting):
    k_total = amp_full.shape[0]
    block_rows = min(512, k_total)
    summed = starting
    for first_row in range(0, k_total, block_rows):
        summed = contract_rows(
            summed,
            amp_full[first_row : first_row + block_rows],
            int_full[first_row : first_row + block_rows],
        )
    return summed


def shards(amplitudes, amp_mask, integrals, int_mask, owner, occ_energy, vir_energy):
    tile_width = TILE
    narrow_count = lax.axis_size("narrow")
    wide_index = lax.axis_index("wide")
    narrow_index = lax.axis_index("narrow")
    src_rows = amplitudes.shape[0]
    occ_all = amplitudes.shape[1]
    occ_here = occ_energy.shape[0]
    vir_here = integrals.shape[1]
    first_src = (wide_index * narrow_count + narrow_index) * src_rows
    src_tiles = (first_src + jnp.arange(src_rows, dtype=jnp.int32)) // tile_width
    src_mask = jnp.take(amp_mask, src_tiles, axis=0)
    src_wide = jnp.broadcast_to(
        src_mask[:, :, None], (src_rows, occ_all // tile_width, tile_width)
    ).reshape(src_rows, occ_all)
    masked = jnp.where(src_wide == 1, amplitudes, jnp.zeros((), amplitudes.dtype))
    vir_tiles_here = vir_here // tile_width
    slot_ids = wide_index * vir_tiles_here + jnp.arange(vir_tiles_here, dtype=jnp.int32)
    tile_ids = jnp.take(owner, slot_ids)
    vir_mask = jnp.take(int_mask, tile_ids, axis=1)
    int_rows = integrals.shape[0]
    row_tiles = int_rows // tile_width
    local_mask = lax.dynamic_slice_in_dim(vir_mask, narrow_index * row_tiles, row_tiles, 0)
    local_wide = jnp.broadcast_to(
        local_mask[:, None, :, None], (row_tiles, tile_width, vir_tiles_here, tile_width)
    ).reshape(int_rows, vir_here)
    int_masked = jnp.where(local_wide == 1, integrals, jnp.zeros((), integrals.dtype))
    int_full = lax.all_gather(int_masked, "narrow", axis=0, tiled=True)
    starting = jnp.zeros((occ_here, vir_here), jnp.float32)
    regrouped = lax.all_to_all(masked, "narrow", split_axis=1, concat_axis=0, tiled=True)
    amp_full = lax.all_gather(regrouped, "wide", axis=0, tiled=True)
    ladder = contract_all(amp_full, int_full, starting)
    vir_energy_here = jnp.take(vir_energy.reshape(-1, tile_width), tile_ids, axis=0).reshape(
        vir_here
    )
    denominator = vir_energy_here[None, :] - occ_energy[:, None]
    return (ladder / denominator).astype(jnp.bfloat16)


MESH = pl.DeviceIdType.MESH
LANES = 128


def lookup(table, z, y):
    value = jnp.int32(table[0][0])
    for zz in range(len(table)):
        for yy in range(2):
            if table[zz][yy] != table[0][0]:
                value = jnp.where((z == zz) & (y == yy), jnp.int32(table[zz][yy]), value)
    return value


ARRIVALS = (
    ("z", 0, 1, 3.5),
    ("x", 0, 0, 3.5),
    ("y", 1, 0, 5.5),
    ("z", 0, 2, 6.5),
    ("x", 0, 1, 7.0),
    ("z", 1, 1, 9.0),
    ("x", 1, 0, 9.5),
    ("z", 0, 3, 10.0),
    ("x", 0, 2, 11.0),
    ("z", 1, 2, 12.0),
    ("x", 1, 1, 14.5),
    ("x", 0, 3, 15.0),
    ("z", 1, 3, 16.0),
    ("x", 1, 2, 18.5),
    ("x", 1, 3, 20.5),
)


def schedule(z_count):
    half = z_count // 2
    event = {(kind, dist): i for i, (kind, cross, dist, _) in enumerate(ARRIVALS) if cross == 1}
    event["z", 0] = event["y", 0]
    chunks = [[None] * 2 for _ in range(z_count)]
    units = [[None] * 2 for _ in range(z_count)]
    place = [0] * (2 * z_count)
    for z in range(z_count):
        for y in range(2):
            groups = sorted(range(y * half, (y + 1) * half), key=lambda g: abs(g - z))
            chunks[z][y] = [(g, e) for g in groups for e in range(2)]
        for y in range(2):
            remote = chunks[z][1 - y]
            rows = []
            for g in range(z_count):
                for e in range(2):
                    at = event["xz"[1 - e], abs(g - z)]
                    n = remote.index((g, e)) if (g, e) in remote else -1
                    ready = max(ARRIVALS[at][3], 8.0 + 5.2 * n)
                    rows.append((ready, at, g, e, n))
            rows.sort()
            units[z][y] = rows
            for i, (ready, at, _, _, _) in enumerate(rows):
                late = [j for j, a in enumerate(ARRIVALS) if a[3] + 1.0 >= ready]
                place[i] = max(place[i], at, late[0] if late else len(ARRIVALS) - 1)
    for i in range(1, len(place)):
        place[i] = max(place[i], place[i - 1])
    return chunks, units, place


def ladder_kernel(
    z_count,
    amp_hbm,
    int_hbm,
    amask_hbm,
    imask_hbm,
    owner_hbm,
    occ_hbm,
    vir_hbm,
    out_ref,
    amp_scr,
    int_scr,
    acc,
    recip,
    amask,
    imask,
    occ_cols,
    amask_ref,
    imask_ref,
    owner_ref,
    occ_ref,
    vir_ref,
    own_sem,
    ycross_send,
    int_send,
    int_recv,
    send_sem,
    recv_sem,
):
    w = lax.axis_index("wide")
    y = lax.axis_index("narrow")
    z, x, c = w // 4, (w // 2) % 2, w % 2
    rows = amp_hbm.shape[0]
    occ_here, vir_here = acc.shape
    unit = int_scr.shape[0] // (2 * z_count)
    half_groups = z_count // 2
    chunks, units, place = schedule(z_count)

    def wide_id(zz, xx, cc):
        return zz * 4 + xx * 2 + cc

    y_peer = (w, 1 - y)
    x_peer = (wide_id(z, 1 - x, c), y)
    c_peer = (wide_id(z, x, 1 - c), y)
    r_peer = (w + 4, y)
    l_peer = (w - 4, y)
    has_r, has_l = z < z_count - 1, z > 0

    barrier = pltpu.get_barrier_semaphore()
    for peer in (y_peer, x_peer, c_peer):
        pl.semaphore_signal(barrier, inc=1, device_id=peer, device_id_type=MESH)

    @pl.when(has_r)
    def _():
        pl.semaphore_signal(barrier, inc=1, device_id=r_peer, device_id_type=MESH)

    @pl.when(has_l)
    def _():
        pl.semaphore_signal(barrier, inc=1, device_id=l_peer, device_id_type=MESH)

    small = [
        pltpu.make_async_copy(src, dst, own_sem.at[2 + i])
        for i, (src, dst) in enumerate(
            (
                (amask_hbm, amask_ref),
                (imask_hbm, imask_ref),
                (owner_hbm, owner_ref),
                (occ_hbm, occ_ref),
                (vir_hbm, vir_ref),
            )
        )
    ]
    for one in small:
        one.start()

    pl.semaphore_wait(barrier, 3 + jnp.where(has_r, 1, 0) + jnp.where(has_l, 1, 0))

    def block_id(zz, xx, cc, h):
        return wide_id(zz, xx, cc) * 2 + h

    def block(zz, xx, cc, h):
        first = pl.multiple_of(block_id(zz, xx, cc, h) * rows, rows)
        return amp_scr.at[pl.ds(first, rows), :]

    def half_cols(yy):
        return amp_hbm.at[:, pl.ds(pl.multiple_of(yy * occ_here, LANES), occ_here)]

    RIGHT, LEFT, ACROSS, CORE, CORE2, RIGHT2, LEFT2 = range(7)
    peers = (r_peer, l_peer, x_peer, c_peer, c_peer, r_peer, l_peer)

    def copy(kind, zz, xx, h, src=None):
        there = block(zz, xx, c, h)
        return pltpu.make_async_remote_copy(
            src_ref=there if src is None else src,
            dst_ref=there,
            send_sem=send_sem.at[kind, zz * 2 + h],
            recv_sem=recv_sem.at[block_id(zz, xx, c, h)],
            device_id=peers[kind],
            device_id_type=MESH,
        )

    def arrived(zz, xx, cc, h):
        here = block(zz, xx, cc, h)
        pltpu.make_async_remote_copy(
            src_ref=here,
            dst_ref=here,
            send_sem=send_sem.at[CORE, zz * 2 + h],
            recv_sem=recv_sem.at[block_id(zz, xx, cc, h)],
            device_id=c_peer,
            device_id_type=MESH,
        ).wait_recv()

    cross = pltpu.make_async_remote_copy(
        src_ref=half_cols(1 - y),
        dst_ref=block(z, x, c, y),
        send_sem=ycross_send,
        recv_sem=recv_sem.at[block_id(z, x, c, y)],
        device_id=y_peer,
        device_id_type=MESH,
    )
    cross.start()

    def spread_own(h, src):
        @pl.when(has_r)
        def _():
            copy(RIGHT, z, x, h, src).start()

        @pl.when(has_l)
        def _():
            copy(LEFT, z, x, h, src).start()

        copy(ACROSS, z, x, h, src).start()
        copy(CORE, z, x, h, src).start()

    spread_own(y, half_cols(y))

    def unit_row(g, far):
        return (g * 2 + x + far - 2 * x * far) * unit

    def int_chunk(n):
        g = lookup([[r[n][0] for r in row] for row in chunks], z, y)
        first = unit_row(g, chunks[0][0][n][1])
        return pltpu.make_async_remote_copy(
            src_ref=int_hbm.at[
                pl.ds(pl.multiple_of(first - y * half_groups * 2 * unit, unit), unit), :
            ],
            dst_ref=int_scr.at[pl.ds(pl.multiple_of(first, unit), unit), :],
            send_sem=int_send.at[n],
            recv_sem=int_recv.at[n],
            device_id=y_peer,
            device_id_type=MESH,
        )

    n_chunks = 2 * half_groups
    int_chunk(0).start()

    own_copy = pltpu.make_async_copy(half_cols(y), block(z, x, c, y), own_sem.at[0])
    own_copy.start()
    kept = half_groups * 2 * unit
    held = pltpu.make_async_copy(
        int_hbm, int_scr.at[pl.ds(pl.multiple_of(y * kept, unit), kept), :], own_sem.at[1]
    )
    held.start()

    slots = vir_here // TILE

    def prepare_masks():
        for one in small:
            one.wait()
        lane = lax.broadcasted_iota(jnp.int32, (1, vir_here), 1) // TILE
        tile_of = jnp.zeros((1, vir_here), jnp.int32)
        for j in range(slots):
            tile_of = jnp.where(lane == j, owner_ref[w * slots + j], tile_of)
        q_tiles = imask_ref.shape[1]
        pick = lax.broadcasted_iota(jnp.int32, (q_tiles, vir_here), 0) == tile_of
        imask[...] = jnp.dot(
            imask_ref[...].astype(jnp.float32).astype(jnp.bfloat16),
            jnp.where(pick, 1.0, 0.0).astype(jnp.bfloat16),
            preferred_element_type=jnp.float32,
        )
        p_tiles = amask_ref.shape[1]
        p_lane = lax.broadcasted_iota(jnp.int32, (p_tiles, occ_here), 1) // TILE
        p_tile = y * (occ_here // TILE) + p_lane
        pick_p = lax.broadcasted_iota(jnp.int32, (p_tiles, occ_here), 0) == p_tile
        amask[...] = jnp.dot(
            amask_ref[...].astype(jnp.float32).astype(jnp.bfloat16),
            jnp.where(pick_p, 1.0, 0.0).astype(jnp.bfloat16),
            preferred_element_type=jnp.float32,
        )

    low = lax.broadcasted_iota(jnp.int32, (1, LANES), 1) < TILE

    def energies(tile, upper):
        row = vir_ref[pl.ds(tile // 2, 1), :]
        turned = jnp.concatenate([row[:, TILE:], row[:, :TILE]], axis=1)
        odd = jnp.full((1, LANES), tile % 2, jnp.int32) == upper
        return jnp.where(odd, row, turned)

    def prepare_reciprocals():
        occ_t = jnp.transpose(occ_ref[...])
        for j in range(occ_here // LANES):
            occ_cols[j * LANES : (j + 1) * LANES, :] = jnp.broadcast_to(
                occ_t[:, j : j + 1], (LANES, LANES)
            )
        for j in range(slots // 2):
            first = energies(owner_ref[w * slots + 2 * j], 0)
            second = energies(owner_ref[w * slots + 2 * j + 1], 1)
            vir_row = jnp.where(low, first, second)

            @pl.loop(0, occ_here // LANES)
            def _(i):
                at = pl.ds(pl.multiple_of(i * LANES, LANES), LANES)
                recip[at, j * LANES : (j + 1) * LANES] = 1.0 / (vir_row - occ_cols[at, :])

    step = 256

    def multiply(i):
        g = lookup([[r[i][2] for r in row] for row in units], z, y)
        far = lookup([[r[i][3] for r in row] for row in units], z, y)
        first_row = unit_row(g, far)
        xx = x + far - 2 * x * far
        for h in range(2):
            arrived(g, xx, 1 - c, h)

        order = [[r[i][4] for r in row] for row in units]
        here = int_scr.at[pl.ds(pl.multiple_of(first_row, unit), unit), :]
        for n in range(n_chunks):
            if any(n in row for row in order):

                @pl.when(lookup(order, z, y) == n)
                def _():
                    pltpu.make_async_remote_copy(
                        src_ref=here,
                        dst_ref=here,
                        send_sem=int_send.at[n],
                        recv_sem=int_recv.at[n],
                        device_id=y_peer,
                        device_id_type=MESH,
                    ).wait_recv()

        tiles = unit // TILE
        for t in range(tiles):
            at = pl.ds(pl.multiple_of(first_row + t * TILE, TILE), TILE)
            row = imask[pl.ds(first_row // TILE + t, 1), :].astype(jnp.bfloat16)
            int_scr[at, :] = int_scr[at, :] * jnp.broadcast_to(row, (TILE, vir_here))

        @pl.loop(0, occ_here // step)
        def _(p):
            cols = pl.ds(pl.multiple_of(p * step, step), step)
            parts = []
            for t in range(tiles):
                at = pl.ds(pl.multiple_of(first_row + t * TILE, TILE), TILE)
                row = amask[pl.ds(first_row // TILE + t, 1), cols].astype(jnp.bfloat16)
                parts.append(amp_scr[at, cols] * jnp.broadcast_to(row, (TILE, step)))
            left = jnp.concatenate(parts, axis=0)
            term = lax.dot_general(
                left,
                int_scr[pl.ds(pl.multiple_of(first_row, unit), unit), :],
                (((0,), (0,)), ((), ())),
                preferred_element_type=jnp.float32,
            )
            if i == 0:
                acc[cols, :] = term
            elif i < 2 * z_count - 1:
                acc[cols, :] += term
            else:
                out_ref[cols, :] = ((acc[cols, :] + term) * recip[cols, :]).astype(jnp.bfloat16)

    def each_side(dist, act):
        if dist == 0:
            act(z, None)
            return

        @pl.when(z - dist >= 0)
        def _():
            act(z - dist, RIGHT)

        @pl.when(z + dist <= z_count - 1)
        def _():
            act(z + dist, LEFT)

    def arrival(kind, h, dist):
        along = h is own_half

        def from_end(zz, onward):
            return zz == (0 if onward == RIGHT else z_count - 1)

        def from_z(zz, onward):
            arrived(zz, x, c, h)

            @pl.when(has_r if onward == RIGHT else has_l)
            def _():
                copy(onward, zz, x, h).start()

            if along and dist >= 2:

                @pl.when(jnp.logical_not(from_end(zz, onward)))
                def _():
                    copy(ACROSS, zz, x, h).start()
            else:
                copy(ACROSS, zz, x, h).start()
            copy(CORE, zz, x, h).start()

        def from_x(zz, onward):
            arrived(zz, 1 - x, c, h)
            if along and 1 <= dist < z_count - 1:

                @pl.when(from_end(zz, onward))
                def _():
                    copy(RIGHT2 if onward == RIGHT else LEFT2, zz, 1 - x, h).start()

            copy(CORE2, zz, 1 - x, h).start()

        if kind == "y":
            arrived(z, x, c, h)
            spread_own(h, block(z, x, c, h))
        else:
            each_side(dist, from_z if kind == "z" else from_x)

    own_half, other_half = y, 1 - y
    sent = 1
    for at, (kind, crossed, dist, when) in enumerate(ARRIVALS):
        arrival(kind, other_half if crossed else own_half, dist)
        if at == 0:
            prepare_masks()
        if kind == "y":
            prepare_reciprocals()
        while sent < n_chunks and when >= 5.2 * (sent - 1) + 4.0:
            if sent >= 2:
                int_chunk(sent - 2).wait_send()
            int_chunk(sent).start()
            sent += 1
        for i in range(2 * z_count):
            if place[i] == at:
                if i == 0:
                    own_copy.wait()
                    held.wait()
                multiply(i)

    cross.wait_send()
    for n in range(n_chunks - 2, n_chunks):
        int_chunk(n).wait_send()
    for zz in range(z_count):
        for h in range(2):

            @pl.when(has_r & (zz <= z))
            def _():
                copy(RIGHT, zz, x, h).wait_send()

            @pl.when(has_l & (zz >= z))
            def _():
                copy(LEFT, zz, x, h).wait_send()

            around = False
            if zz == 0:
                around = (h == own_half) & (z >= 2)
            elif zz == z_count - 1:
                around = (h == own_half) & (z <= z_count - 3)
            if around is False:
                copy(ACROSS, zz, x, h).wait_send()
            else:

                @pl.when(jnp.logical_not(around))
                def _():
                    copy(ACROSS, zz, x, h).wait_send()

            copy(CORE, zz, x, h).wait_send()
            copy(CORE2, zz, 1 - x, h).wait_send()

    @pl.when(has_r & has_l)
    def _():
        copy(RIGHT2, 0, 1 - x, own_half).wait_send()
        copy(LEFT2, z_count - 1, 1 - x, own_half).wait_send()


def relayed(amplitudes, amp_mask, integrals, int_mask, owner, occ_energy, vir_energy):
    z_count = lax.axis_size("wide") // 4
    k_total = amplitudes.shape[0] * lax.axis_size("wide") * 2
    occ_here, vir_here = occ_energy.shape[0], integrals.shape[1]
    hbm = pl.BlockSpec(memory_space=pltpu.HBM)
    dma = pltpu.SemaphoreType.DMA
    occ_rows, vir_rows = occ_here // LANES, vir_energy.shape[0] // LANES
    return pl.pallas_call(
        functools.partial(ladder_kernel, z_count),
        out_shape=jax.ShapeDtypeStruct((occ_here, vir_here), jnp.bfloat16),
        in_specs=[hbm] * 7,
        out_specs=pl.BlockSpec(memory_space=pltpu.VMEM),
        scratch_shapes=[
            pltpu.VMEM((k_total, occ_here), jnp.bfloat16),
            pltpu.VMEM((k_total, vir_here), jnp.bfloat16),
            pltpu.VMEM((occ_here, vir_here), jnp.float32),
            pltpu.VMEM((occ_here, vir_here), jnp.float32),
            pltpu.VMEM((k_total // TILE, occ_here), jnp.float32),
            pltpu.VMEM((k_total // TILE, vir_here), jnp.float32),
            pltpu.VMEM((occ_here, LANES), jnp.float32),
            pltpu.VMEM(amp_mask.shape, jnp.int32),
            pltpu.VMEM(int_mask.shape, jnp.int32),
            pltpu.SMEM(owner.shape, jnp.int32),
            pltpu.VMEM((occ_rows, LANES), jnp.float32),
            pltpu.VMEM((vir_rows, LANES), jnp.float32),
            dma((7,)),
            dma,
            dma((z_count,)),
            dma((z_count,)),
            dma((7, 2 * z_count)),
            dma((8 * z_count,)),
        ],
        compiler_params=pltpu.CompilerParams(
            collective_id=0, has_side_effects=True, vmem_limit_bytes=40 * 2**20
        ),
        cost_estimate=pl.CostEstimate(
            flops=2 * k_total * occ_here * vir_here, bytes_accessed=4 * 2**20, transcendentals=0
        ),
    )(
        *(
            pltpu.with_memory_space_constraint(one, pltpu.HBM)
            for one in (
                amplitudes,
                integrals,
                amp_mask,
                int_mask,
                owner,
                occ_energy.reshape(-1, LANES),
                vir_energy.reshape(-1, LANES),
            )
        )
    )


def fits(mesh, amplitudes, integrals):
    wide, narrow = mesh.shape["wide"], mesh.shape["narrow"]
    return (
        narrow == 2
        and wide == 16
        and amplitudes.shape[0] == wide * narrow * TILE
        and amplitudes.shape[1] % (2 * 1024) == 0
        and (integrals.shape[1] // wide) % LANES == 0
    )


def solution(mesh):
    def run(amplitudes, amp_mask, integrals, int_mask, owner, occ_energy, vir_energy):
        body = relayed if fits(mesh, amplitudes, integrals) else shards
        return jax.shard_map(
            body,
            mesh=mesh,
            in_specs=(
                P(("wide", "narrow"), None),
                P(),
                P("narrow", "wide"),
                P(),
                P(),
                P("narrow"),
                P(),
            ),
            out_specs=P("narrow", "wide"),
            check_vma=False,
        )(amplitudes, amp_mask, integrals, int_mask, owner, occ_energy, vir_energy)

    return run
```

```python
import functools

import jax
import jax.numpy as jnp
from jax import lax
from jax.experimental import pallas as pl
from jax.experimental.pallas import tpu as pltpu
from jax.sharding import PartitionSpec as P

TILE = 64


def contract_rows(summed, rows_in, int_part):
    return summed + lax.dot_general(
        rows_in, int_part, (((0,), (0,)), ((), ())), preferred_element_type=jnp.float32
    )


def contract_all(amp_full, int_full, starting):
    k_total = amp_full.shape[0]
    block_rows = min(512, k_total)
    summed = starting
    for first_row in range(0, k_total, block_rows):
        summed = contract_rows(
            summed,
            amp_full[first_row : first_row + block_rows],
            int_full[first_row : first_row + block_rows],
        )
    return summed


def shards(amplitudes, amp_mask, integrals, int_mask, owner, occ_energy, vir_energy):
    tile_width = TILE
    narrow_count = lax.axis_size("narrow")
    wide_index = lax.axis_index("wide")
    narrow_index = lax.axis_index("narrow")
    src_rows = amplitudes.shape[0]
    occ_all = amplitudes.shape[1]
    occ_here = occ_energy.shape[0]
    vir_here = integrals.shape[1]
    first_src = (wide_index * narrow_count + narrow_index) * src_rows
    src_tiles = (first_src + jnp.arange(src_rows, dtype=jnp.int32)) // tile_width
    src_mask = jnp.take(amp_mask, src_tiles, axis=0)
    src_wide = jnp.broadcast_to(
        src_mask[:, :, None], (src_rows, occ_all // tile_width, tile_width)
    ).reshape(src_rows, occ_all)
    masked = jnp.where(src_wide == 1, amplitudes, jnp.zeros((), amplitudes.dtype))
    vir_tiles_here = vir_here // tile_width
    slot_ids = wide_index * vir_tiles_here + jnp.arange(vir_tiles_here, dtype=jnp.int32)
    tile_ids = jnp.take(owner, slot_ids)
    vir_mask = jnp.take(int_mask, tile_ids, axis=1)
    int_rows = integrals.shape[0]
    row_tiles = int_rows // tile_width
    local_mask = lax.dynamic_slice_in_dim(vir_mask, narrow_index * row_tiles, row_tiles, 0)
    local_wide = jnp.broadcast_to(
        local_mask[:, None, :, None], (row_tiles, tile_width, vir_tiles_here, tile_width)
    ).reshape(int_rows, vir_here)
    int_masked = jnp.where(local_wide == 1, integrals, jnp.zeros((), integrals.dtype))
    int_full = lax.all_gather(int_masked, "narrow", axis=0, tiled=True)
    starting = jnp.zeros((occ_here, vir_here), jnp.float32)
    regrouped = lax.all_to_all(masked, "narrow", split_axis=1, concat_axis=0, tiled=True)
    amp_full = lax.all_gather(regrouped, "wide", axis=0, tiled=True)
    ladder = contract_all(amp_full, int_full, starting)
    vir_energy_here = jnp.take(vir_energy.reshape(-1, tile_width), tile_ids, axis=0).reshape(
        vir_here
    )
    denominator = vir_energy_here[None, :] - occ_energy[:, None]
    return (ladder / denominator).astype(jnp.bfloat16)


MESH = pl.DeviceIdType.MESH
LANES = 128


def lookup(table, z, y):
    value = jnp.int32(table[0][0])
    for zz in range(len(table)):
        for yy in range(2):
            if table[zz][yy] != table[0][0]:
                value = jnp.where((z == zz) & (y == yy), jnp.int32(table[zz][yy]), value)
    return value


ARRIVALS = (
    ("z", 0, 1, 3.5),
    ("x", 0, 0, 3.5),
    ("y", 1, 0, 5.5),
    ("z", 0, 2, 6.5),
    ("x", 0, 1, 7.0),
    ("z", 1, 1, 9.0),
    ("x", 1, 0, 9.5),
    ("z", 0, 3, 10.0),
    ("z", 1, 2, 12.0),
    ("x", 0, 2, 12.0),
    ("x", 1, 1, 14.5),
    ("z", 1, 3, 16.0),
    ("x", 0, 3, 18.0),
    ("x", 1, 2, 18.5),
    ("x", 1, 3, 20.5),
)


def schedule(z_count):
    half = z_count // 2
    event = {(kind, dist): i for i, (kind, cross, dist, _) in enumerate(ARRIVALS) if cross == 1}
    event["z", 0] = event["y", 0]
    chunks = [[None] * 2 for _ in range(z_count)]
    units = [[None] * 2 for _ in range(z_count)]
    place = [0] * (2 * z_count)
    for z in range(z_count):
        for y in range(2):
            groups = sorted(range(y * half, (y + 1) * half), key=lambda g: abs(g - z))
            chunks[z][y] = [(g, e) for g in groups for e in range(2)]
        for y in range(2):
            remote = chunks[z][1 - y]
            rows = []
            for g in range(z_count):
                for e in range(2):
                    at = event["xz"[1 - e], abs(g - z)]
                    n = remote.index((g, e)) if (g, e) in remote else -1
                    ready = max(ARRIVALS[at][3], 8.0 + 5.2 * n)
                    rows.append((ready, at, g, e, n))
            rows.sort()
            units[z][y] = rows
            for i, (ready, at, _, _, _) in enumerate(rows):
                late = [j for j, a in enumerate(ARRIVALS) if a[3] + 1.0 >= ready]
                place[i] = max(place[i], at, late[0] if late else len(ARRIVALS) - 1)
    for i in range(1, len(place)):
        place[i] = max(place[i], place[i - 1])
    return chunks, units, place


def ladder_kernel(
    z_count,
    amp_hbm,
    int_hbm,
    amask_hbm,
    imask_hbm,
    owner_hbm,
    occ_hbm,
    vir_hbm,
    out_ref,
    amp_scr,
    int_scr,
    acc,
    recip,
    amask,
    imask,
    occ_cols,
    amask_ref,
    imask_ref,
    owner_ref,
    occ_ref,
    vir_ref,
    turned,
    own_sem,
    ycross_send,
    int_send,
    int_recv,
    send_sem,
    recv_sem,
):
    w = lax.axis_index("wide")
    y = lax.axis_index("narrow")
    z, x, c = w // 4, (w // 2) % 2, w % 2
    rows = amp_hbm.shape[0]
    occ_here, vir_here = acc.shape
    unit = int_scr.shape[0] // (2 * z_count)
    half_groups = z_count // 2
    chunks, units, place = schedule(z_count)

    def wide_id(zz, xx, cc):
        return zz * 4 + xx * 2 + cc

    y_peer = (w, 1 - y)
    x_peer = (wide_id(z, 1 - x, c), y)
    c_peer = (wide_id(z, x, 1 - c), y)
    r_peer = (w + 4, y)
    l_peer = (w - 4, y)
    has_r, has_l = z < z_count - 1, z > 0

    barrier = pltpu.get_barrier_semaphore()
    for peer in (y_peer, x_peer, c_peer):
        pl.semaphore_signal(barrier, inc=1, device_id=peer, device_id_type=MESH)

    @pl.when(has_r)
    def _():
        pl.semaphore_signal(barrier, inc=1, device_id=r_peer, device_id_type=MESH)

    @pl.when(has_l)
    def _():
        pl.semaphore_signal(barrier, inc=1, device_id=l_peer, device_id_type=MESH)

    small = [
        pltpu.make_async_copy(src, dst, own_sem.at[2 + i])
        for i, (src, dst) in enumerate(
            (
                (amask_hbm, amask_ref),
                (imask_hbm, imask_ref),
                (owner_hbm, owner_ref),
                (occ_hbm, occ_ref),
                (vir_hbm, vir_ref),
            )
        )
    ]
    for one in small:
        one.start()

    pl.semaphore_wait(barrier, 3 + jnp.where(has_r, 1, 0) + jnp.where(has_l, 1, 0))

    def block_id(zz, xx, cc, h):
        return wide_id(zz, xx, cc) * 2 + h

    def block(zz, xx, cc, h):
        first = pl.multiple_of(block_id(zz, xx, cc, h) * rows, rows)
        return amp_scr.at[pl.ds(first, rows), :]

    def half_cols(yy):
        return amp_hbm.at[:, pl.ds(pl.multiple_of(yy * occ_here, LANES), occ_here)]

    RIGHT, LEFT, ACROSS, CORE, CORE2, RIGHT2, LEFT2 = range(7)
    peers = (r_peer, l_peer, x_peer, c_peer, c_peer, r_peer, l_peer)

    def copy(kind, zz, xx, h, src=None):
        there = block(zz, xx, c, h)
        return pltpu.make_async_remote_copy(
            src_ref=there if src is None else src,
            dst_ref=there,
            send_sem=send_sem.at[kind, zz * 2 + h],
            recv_sem=recv_sem.at[block_id(zz, xx, c, h)],
            device_id=peers[kind],
            device_id_type=MESH,
        )

    def arrived(zz, xx, cc, h):
        here = block(zz, xx, cc, h)
        pltpu.make_async_remote_copy(
            src_ref=here,
            dst_ref=here,
            send_sem=send_sem.at[CORE, zz * 2 + h],
            recv_sem=recv_sem.at[block_id(zz, xx, cc, h)],
            device_id=c_peer,
            device_id_type=MESH,
        ).wait_recv()

    cross = pltpu.make_async_remote_copy(
        src_ref=half_cols(1 - y),
        dst_ref=block(z, x, c, y),
        send_sem=ycross_send,
        recv_sem=recv_sem.at[block_id(z, x, c, y)],
        device_id=y_peer,
        device_id_type=MESH,
    )
    cross.start()

    def spread_own(h, src):
        @pl.when(has_r)
        def _():
            copy(RIGHT, z, x, h, src).start()

        @pl.when(has_l)
        def _():
            copy(LEFT, z, x, h, src).start()

        copy(ACROSS, z, x, h, src).start()
        copy(CORE, z, x, h, src).start()

    spread_own(y, half_cols(y))

    def unit_row(g, far):
        return (g * 2 + x + far - 2 * x * far) * unit

    def int_chunk(n):
        g = lookup([[r[n][0] for r in row] for row in chunks], z, y)
        first = unit_row(g, chunks[0][0][n][1])
        return pltpu.make_async_remote_copy(
            src_ref=int_hbm.at[
                pl.ds(pl.multiple_of(first - y * half_groups * 2 * unit, unit), unit), :
            ],
            dst_ref=int_scr.at[pl.ds(pl.multiple_of(first, unit), unit), :],
            send_sem=int_send.at[n],
            recv_sem=int_recv.at[n],
            device_id=y_peer,
            device_id_type=MESH,
        )

    n_chunks = 2 * half_groups

    own_copy = pltpu.make_async_copy(half_cols(y), block(z, x, c, y), own_sem.at[0])
    own_copy.start()
    kept = half_groups * 2 * unit
    held = pltpu.make_async_copy(
        int_hbm, int_scr.at[pl.ds(pl.multiple_of(y * kept, unit), kept), :], own_sem.at[1]
    )
    held.start()

    slots = vir_here // TILE

    def prepare_masks():
        for one in small:
            one.wait()
        lane = lax.broadcasted_iota(jnp.int32, (1, vir_here), 1) // TILE
        tile_of = jnp.zeros((1, vir_here), jnp.int32)
        for j in range(slots):
            tile_of = jnp.where(lane == j, owner_ref[w * slots + j], tile_of)
        q_tiles = imask_ref.shape[1]
        pick = lax.broadcasted_iota(jnp.int32, (q_tiles, vir_here), 0) == tile_of
        imask[...] = jnp.dot(
            imask_ref[...].astype(jnp.float32).astype(jnp.bfloat16),
            jnp.where(pick, 1.0, 0.0).astype(jnp.bfloat16),
            preferred_element_type=jnp.float32,
        )
        p_tiles = amask_ref.shape[1]
        p_lane = lax.broadcasted_iota(jnp.int32, (p_tiles, occ_here), 1) // TILE
        p_tile = y * (occ_here // TILE) + p_lane
        pick_p = lax.broadcasted_iota(jnp.int32, (p_tiles, occ_here), 0) == p_tile
        amask[...] = jnp.dot(
            amask_ref[...].astype(jnp.float32).astype(jnp.bfloat16),
            jnp.where(pick_p, 1.0, 0.0).astype(jnp.bfloat16),
            preferred_element_type=jnp.float32,
        )

    low = lax.broadcasted_iota(jnp.int32, (1, LANES), 1) < TILE

    def energies(tile, upper):
        row = vir_ref[pl.ds(tile // 2, 1), :]
        swapped = jnp.concatenate([row[:, TILE:], row[:, :TILE]], axis=1)
        odd = jnp.full((1, LANES), tile % 2, jnp.int32) == upper
        return jnp.where(odd, row, swapped)

    def prepare_reciprocals():
        occ_t = jnp.transpose(occ_ref[...])
        for j in range(occ_here // LANES):
            occ_cols[j * LANES : (j + 1) * LANES, :] = jnp.broadcast_to(
                occ_t[:, j : j + 1], (LANES, LANES)
            )
        for j in range(slots // 2):
            first = energies(owner_ref[w * slots + 2 * j], 0)
            second = energies(owner_ref[w * slots + 2 * j + 1], 1)
            vir_row = jnp.where(low, first, second)

            @pl.loop(0, occ_here // LANES)
            def _(i):
                at = pl.ds(pl.multiple_of(i * LANES, LANES), LANES)
                recip[at, j * LANES : (j + 1) * LANES] = 1.0 / (vir_row - occ_cols[at, :])

    step = 256

    def multiply(i):
        g = lookup([[r[i][2] for r in row] for row in units], z, y)
        far = lookup([[r[i][3] for r in row] for row in units], z, y)
        first_row = unit_row(g, far)
        xx = x + far - 2 * x * far
        for h in range(2):
            arrived(g, xx, 1 - c, h)

        tiles = unit // TILE
        last = i == 2 * z_count - 1

        def masked_amplitudes(cols):
            parts = []
            for t in range(tiles):
                at = pl.ds(pl.multiple_of(first_row + t * TILE, TILE), TILE)
                row = amask[pl.ds(first_row // TILE + t, 1), cols].astype(jnp.bfloat16)
                parts.append(amp_scr[at, cols] * jnp.broadcast_to(row, (TILE, step)))
            return jnp.concatenate(parts, axis=0)

        if last:
            for p in range(occ_here // step):
                cols = pl.ds(p * step, step)
                turned[cols, :] = jnp.transpose(masked_amplitudes(cols))

        order = [[r[i][4] for r in row] for row in units]
        here = int_scr.at[pl.ds(pl.multiple_of(first_row, unit), unit), :]
        for n in range(n_chunks):
            if any(n in row for row in order):

                @pl.when(lookup(order, z, y) == n)
                def _():
                    pltpu.make_async_remote_copy(
                        src_ref=here,
                        dst_ref=here,
                        send_sem=int_send.at[n],
                        recv_sem=int_recv.at[n],
                        device_id=y_peer,
                        device_id_type=MESH,
                    ).wait_recv()

        for t in range(tiles):
            at = pl.ds(pl.multiple_of(first_row + t * TILE, TILE), TILE)
            row = imask[pl.ds(first_row // TILE + t, 1), :].astype(jnp.bfloat16)
            int_scr[at, :] = int_scr[at, :] * jnp.broadcast_to(row, (TILE, vir_here))

        if last:
            right = int_scr[pl.ds(pl.multiple_of(first_row, unit), unit), :]
            for p in range(occ_here // step):
                cols = pl.ds(p * step, step)
                term = jnp.dot(turned[cols, :], right, preferred_element_type=jnp.float32)
                out_ref[cols, :] = ((acc[cols, :] + term) * recip[cols, :]).astype(jnp.bfloat16)
            return

        @pl.loop(0, occ_here // step)
        def _(p):
            cols = pl.ds(pl.multiple_of(p * step, step), step)
            term = lax.dot_general(
                masked_amplitudes(cols),
                int_scr[pl.ds(pl.multiple_of(first_row, unit), unit), :],
                (((0,), (0,)), ((), ())),
                preferred_element_type=jnp.float32,
            )
            if i == 0:
                acc[cols, :] = term
            else:
                acc[cols, :] += term

    def each_side(dist, act):
        if dist == 0:
            act(z, None)
            return

        @pl.when(z - dist >= 0)
        def _():
            act(z - dist, RIGHT)

        @pl.when(z + dist <= z_count - 1)
        def _():
            act(z + dist, LEFT)

    def arrival(kind, h, dist):
        along = h is own_half

        def from_end(zz, onward):
            return zz == (0 if onward == RIGHT else z_count - 1)

        def from_z(zz, onward):
            arrived(zz, x, c, h)

            @pl.when(has_r if onward == RIGHT else has_l)
            def _():
                copy(onward, zz, x, h).start()

            if along and dist >= 2:

                @pl.when(jnp.logical_not(from_end(zz, onward)))
                def _():
                    copy(ACROSS, zz, x, h).start()
            else:
                copy(ACROSS, zz, x, h).start()
            copy(CORE, zz, x, h).start()

        def from_x(zz, onward):
            arrived(zz, 1 - x, c, h)
            if along and 1 <= dist < z_count - 1:

                @pl.when(from_end(zz, onward))
                def _():
                    copy(RIGHT2 if onward == RIGHT else LEFT2, zz, 1 - x, h).start()

            copy(CORE2, zz, 1 - x, h).start()

        if kind == "y":
            arrived(z, x, c, h)
            spread_own(h, block(z, x, c, h))
        else:
            each_side(dist, from_z if kind == "z" else from_x)

    own_half, other_half = y, 1 - y
    prepare_masks()
    int_chunk(0).start()
    sent = 1
    for at, (kind, crossed, dist, when) in enumerate(ARRIVALS):
        arrival(kind, other_half if crossed else own_half, dist)
        if kind == "y":
            prepare_reciprocals()
        while sent < n_chunks and when >= 5.2 * (sent - 1) + 4.0:
            if sent >= 2:
                int_chunk(sent - 2).wait_send()
            int_chunk(sent).start()
            sent += 1
        for i in range(2 * z_count):
            if place[i] == at:
                if i == 0:
                    own_copy.wait()
                    held.wait()
                multiply(i)

    cross.wait_send()
    for n in range(n_chunks - 2, n_chunks):
        int_chunk(n).wait_send()
    for zz in range(z_count):
        for h in range(2):

            @pl.when(has_r & (zz <= z))
            def _():
                copy(RIGHT, zz, x, h).wait_send()

            @pl.when(has_l & (zz >= z))
            def _():
                copy(LEFT, zz, x, h).wait_send()

            around = False
            if zz == 0:
                around = (h == own_half) & (z >= 2)
            elif zz == z_count - 1:
                around = (h == own_half) & (z <= z_count - 3)
            if around is False:
                copy(ACROSS, zz, x, h).wait_send()
            else:

                @pl.when(jnp.logical_not(around))
                def _():
                    copy(ACROSS, zz, x, h).wait_send()

            copy(CORE, zz, x, h).wait_send()
            copy(CORE2, zz, 1 - x, h).wait_send()

    @pl.when(has_r & has_l)
    def _():
        copy(RIGHT2, 0, 1 - x, own_half).wait_send()
        copy(LEFT2, z_count - 1, 1 - x, own_half).wait_send()


def relayed(amplitudes, amp_mask, integrals, int_mask, owner, occ_energy, vir_energy):
    z_count = lax.axis_size("wide") // 4
    k_total = amplitudes.shape[0] * lax.axis_size("wide") * 2
    occ_here, vir_here = occ_energy.shape[0], integrals.shape[1]
    hbm = pl.BlockSpec(memory_space=pltpu.HBM)
    dma = pltpu.SemaphoreType.DMA
    occ_rows, vir_rows = occ_here // LANES, vir_energy.shape[0] // LANES
    return pl.pallas_call(
        functools.partial(ladder_kernel, z_count),
        out_shape=jax.ShapeDtypeStruct((occ_here, vir_here), jnp.bfloat16),
        in_specs=[hbm] * 7,
        out_specs=pl.BlockSpec(memory_space=pltpu.VMEM),
        scratch_shapes=[
            pltpu.VMEM((k_total, occ_here), jnp.bfloat16),
            pltpu.VMEM((k_total, vir_here), jnp.bfloat16),
            pltpu.VMEM((occ_here, vir_here), jnp.float32),
            pltpu.VMEM((occ_here, vir_here), jnp.float32),
            pltpu.VMEM((k_total // TILE, occ_here), jnp.float32),
            pltpu.VMEM((k_total // TILE, vir_here), jnp.float32),
            pltpu.VMEM((occ_here, LANES), jnp.float32),
            pltpu.VMEM(amp_mask.shape, jnp.int32),
            pltpu.VMEM(int_mask.shape, jnp.int32),
            pltpu.SMEM(owner.shape, jnp.int32),
            pltpu.VMEM((occ_rows, LANES), jnp.float32),
            pltpu.VMEM((vir_rows, LANES), jnp.float32),
            pltpu.VMEM((occ_here, k_total // (2 * z_count)), jnp.bfloat16),
            dma((7,)),
            dma,
            dma((z_count,)),
            dma((z_count,)),
            dma((7, 2 * z_count)),
            dma((8 * z_count,)),
        ],
        compiler_params=pltpu.CompilerParams(
            collective_id=0, has_side_effects=True, vmem_limit_bytes=40 * 2**20
        ),
        cost_estimate=pl.CostEstimate(
            flops=2 * k_total * occ_here * vir_here, bytes_accessed=4 * 2**20, transcendentals=0
        ),
    )(
        *(
            pltpu.with_memory_space_constraint(one, pltpu.HBM)
            for one in (
                amplitudes,
                integrals,
                amp_mask,
                int_mask,
                owner,
                occ_energy.reshape(-1, LANES),
                vir_energy.reshape(-1, LANES),
            )
        )
    )


def fits(mesh, amplitudes, integrals):
    wide, narrow = mesh.shape["wide"], mesh.shape["narrow"]
    return (
        narrow == 2
        and wide == 16
        and amplitudes.shape[0] == wide * narrow * TILE
        and amplitudes.shape[1] % (2 * 1024) == 0
        and (integrals.shape[1] // wide) % LANES == 0
    )


def solution(mesh):
    def run(amplitudes, amp_mask, integrals, int_mask, owner, occ_energy, vir_energy):
        body = relayed if fits(mesh, amplitudes, integrals) else shards
        return jax.shard_map(
            body,
            mesh=mesh,
            in_specs=(
                P(("wide", "narrow"), None),
                P(),
                P("narrow", "wide"),
                P(),
                P(),
                P("narrow"),
                P(),
            ),
            out_specs=P("narrow", "wide"),
            check_vma=False,
        )(amplitudes, amp_mask, integrals, int_mask, owner, occ_energy, vir_energy)

    return run
```

```python
import functools

import jax
import jax.numpy as jnp
from jax import lax
from jax.experimental import pallas as pl
from jax.experimental.pallas import tpu as pltpu
from jax.sharding import PartitionSpec as P

TILE = 64


def contract_rows(summed, rows_in, int_part):
    return summed + lax.dot_general(
        rows_in, int_part, (((0,), (0,)), ((), ())), preferred_element_type=jnp.float32
    )


def contract_all(amp_full, int_full, starting):
    k_total = amp_full.shape[0]
    block_rows = min(512, k_total)
    summed = starting
    for first_row in range(0, k_total, block_rows):
        summed = contract_rows(
            summed,
            amp_full[first_row : first_row + block_rows],
            int_full[first_row : first_row + block_rows],
        )
    return summed


def shards(amplitudes, amp_mask, integrals, int_mask, owner, occ_energy, vir_energy):
    tile_width = TILE
    narrow_count = lax.axis_size("narrow")
    wide_index = lax.axis_index("wide")
    narrow_index = lax.axis_index("narrow")
    src_rows = amplitudes.shape[0]
    occ_all = amplitudes.shape[1]
    occ_here = occ_energy.shape[0]
    vir_here = integrals.shape[1]
    first_src = (wide_index * narrow_count + narrow_index) * src_rows
    src_tiles = (first_src + jnp.arange(src_rows, dtype=jnp.int32)) // tile_width
    src_mask = jnp.take(amp_mask, src_tiles, axis=0)
    src_wide = jnp.broadcast_to(
        src_mask[:, :, None], (src_rows, occ_all // tile_width, tile_width)
    ).reshape(src_rows, occ_all)
    masked = jnp.where(src_wide == 1, amplitudes, jnp.zeros((), amplitudes.dtype))
    vir_tiles_here = vir_here // tile_width
    slot_ids = wide_index * vir_tiles_here + jnp.arange(vir_tiles_here, dtype=jnp.int32)
    tile_ids = jnp.take(owner, slot_ids)
    vir_mask = jnp.take(int_mask, tile_ids, axis=1)
    int_rows = integrals.shape[0]
    row_tiles = int_rows // tile_width
    local_mask = lax.dynamic_slice_in_dim(vir_mask, narrow_index * row_tiles, row_tiles, 0)
    local_wide = jnp.broadcast_to(
        local_mask[:, None, :, None], (row_tiles, tile_width, vir_tiles_here, tile_width)
    ).reshape(int_rows, vir_here)
    int_masked = jnp.where(local_wide == 1, integrals, jnp.zeros((), integrals.dtype))
    int_full = lax.all_gather(int_masked, "narrow", axis=0, tiled=True)
    starting = jnp.zeros((occ_here, vir_here), jnp.float32)
    regrouped = lax.all_to_all(masked, "narrow", split_axis=1, concat_axis=0, tiled=True)
    amp_full = lax.all_gather(regrouped, "wide", axis=0, tiled=True)
    ladder = contract_all(amp_full, int_full, starting)
    vir_energy_here = jnp.take(vir_energy.reshape(-1, tile_width), tile_ids, axis=0).reshape(
        vir_here
    )
    denominator = vir_energy_here[None, :] - occ_energy[:, None]
    return (ladder / denominator).astype(jnp.bfloat16)


MESH = pl.DeviceIdType.MESH
LANES = 128


def lookup(table, z, y):
    value = jnp.int32(table[0][0])
    for zz in range(len(table)):
        for yy in range(2):
            if table[zz][yy] != table[0][0]:
                value = jnp.where((z == zz) & (y == yy), jnp.int32(table[zz][yy]), value)
    return value


ARRIVALS = (
    ("z", 0, 1, 3.5),
    ("x", 0, 0, 3.5),
    ("y", 1, 0, 5.5),
    ("z", 0, 2, 6.5),
    ("x", 0, 1, 7.0),
    ("z", 1, 1, 9.0),
    ("x", 1, 0, 9.5),
    ("z", 1, 2, 12.0),
    ("late", 0, 2, 12.0),
    ("x", 0, 2, 12.0),
    ("z", 1, 3, 14.5),
    ("x", 1, 1, 14.5),
    ("z", 0, 3, 17.0),
    ("x", 1, 2, 18.5),
    ("x", 1, 3, 19.5),
    ("x", 0, 3, 19.5),
)


def schedule(z_count):
    half = z_count // 2
    event = {(kind, dist): i for i, (kind, _, dist, _) in enumerate(ARRIVALS)}
    event["z", 0] = event["y", 0]
    chunks = [[None] * 2 for _ in range(z_count)]
    units = [[None] * 2 for _ in range(z_count)]
    place = [0] * (2 * z_count)
    for z in range(z_count):
        for y in range(2):
            groups = sorted(range(y * half, (y + 1) * half), key=lambda g: abs(g - z))
            chunks[z][y] = [(g, e) for g in groups for e in range(2)]
        for y in range(2):
            remote = chunks[z][1 - y]
            rows = []
            for g in range(z_count):
                for e in range(2):
                    at = event["xz"[1 - e], abs(g - z)]
                    n = remote.index((g, e)) if (g, e) in remote else -1
                    ready = max(ARRIVALS[at][3], 8.0 + 5.2 * n)
                    rows.append((ready, at, g, e, n))
            rows.sort()
            units[z][y] = rows
            for i, (ready, at, _, _, _) in enumerate(rows):
                late = [j for j, a in enumerate(ARRIVALS) if a[3] + 1.0 >= ready]
                place[i] = max(place[i], at, late[0] if late else len(ARRIVALS) - 1)
    for i in range(1, len(place)):
        place[i] = max(place[i], place[i - 1])
    return chunks, units, place


def ladder_kernel(
    z_count,
    amp_hbm,
    int_hbm,
    amask_hbm,
    imask_hbm,
    owner_hbm,
    occ_hbm,
    vir_hbm,
    out_ref,
    amp_scr,
    int_scr,
    acc,
    recip,
    amask,
    imask,
    occ_cols,
    amask_ref,
    imask_ref,
    owner_ref,
    occ_ref,
    vir_ref,
    turned,
    own_sem,
    ycross_send,
    int_send,
    int_recv,
    send_sem,
    recv_sem,
):
    w = lax.axis_index("wide")
    y = lax.axis_index("narrow")
    z, x, c = w // 4, (w // 2) % 2, w % 2
    rows = amp_hbm.shape[0]
    occ_here, vir_here = acc.shape
    unit = int_scr.shape[0] // (2 * z_count)
    half_groups = z_count // 2
    chunks, units, place = schedule(z_count)

    def wide_id(zz, xx, cc):
        return zz * 4 + xx * 2 + cc

    y_peer = (w, 1 - y)
    x_peer = (wide_id(z, 1 - x, c), y)
    c_peer = (wide_id(z, x, 1 - c), y)
    r_peer = (w + 4, y)
    l_peer = (w - 4, y)
    has_r, has_l = z < z_count - 1, z > 0

    barrier = pltpu.get_barrier_semaphore()
    for peer in (y_peer, x_peer, c_peer):
        pl.semaphore_signal(barrier, inc=1, device_id=peer, device_id_type=MESH)

    @pl.when(has_r)
    def _():
        pl.semaphore_signal(barrier, inc=1, device_id=r_peer, device_id_type=MESH)

    @pl.when(has_l)
    def _():
        pl.semaphore_signal(barrier, inc=1, device_id=l_peer, device_id_type=MESH)

    small = [
        pltpu.make_async_copy(src, dst, own_sem.at[2 + i])
        for i, (src, dst) in enumerate(
            (
                (amask_hbm, amask_ref),
                (imask_hbm, imask_ref),
                (owner_hbm, owner_ref),
                (occ_hbm, occ_ref),
                (vir_hbm, vir_ref),
            )
        )
    ]
    for one in small:
        one.start()

    pl.semaphore_wait(barrier, 3 + jnp.where(has_r, 1, 0) + jnp.where(has_l, 1, 0))

    def block_id(zz, xx, cc, h):
        return wide_id(zz, xx, cc) * 2 + h

    def block(zz, xx, cc, h):
        first = pl.multiple_of(block_id(zz, xx, cc, h) * rows, rows)
        return amp_scr.at[pl.ds(first, rows), :]

    def half_cols(yy):
        return amp_hbm.at[:, pl.ds(pl.multiple_of(yy * occ_here, LANES), occ_here)]

    RIGHT, LEFT, ACROSS, CORE, CORE2, RIGHT2, LEFT2 = range(7)
    peers = (r_peer, l_peer, x_peer, c_peer, c_peer, r_peer, l_peer)

    def copy(kind, zz, xx, h, src=None):
        there = block(zz, xx, c, h)
        return pltpu.make_async_remote_copy(
            src_ref=there if src is None else src,
            dst_ref=there,
            send_sem=send_sem.at[kind, zz * 2 + h],
            recv_sem=recv_sem.at[block_id(zz, xx, c, h)],
            device_id=peers[kind],
            device_id_type=MESH,
        )

    def arrived(zz, xx, cc, h):
        here = block(zz, xx, cc, h)
        pltpu.make_async_remote_copy(
            src_ref=here,
            dst_ref=here,
            send_sem=send_sem.at[CORE, zz * 2 + h],
            recv_sem=recv_sem.at[block_id(zz, xx, cc, h)],
            device_id=c_peer,
            device_id_type=MESH,
        ).wait_recv()

    cross = pltpu.make_async_remote_copy(
        src_ref=half_cols(1 - y),
        dst_ref=block(z, x, c, y),
        send_sem=ycross_send,
        recv_sem=recv_sem.at[block_id(z, x, c, y)],
        device_id=y_peer,
        device_id_type=MESH,
    )
    cross.start()

    def spread_own(h, src):
        @pl.when(has_r)
        def _():
            copy(RIGHT, z, x, h, src).start()

        @pl.when(has_l)
        def _():
            copy(LEFT, z, x, h, src).start()

        copy(ACROSS, z, x, h, src).start()
        copy(CORE, z, x, h, src).start()

    spread_own(y, half_cols(y))

    def unit_row(g, far):
        return (g * 2 + x + far - 2 * x * far) * unit

    def int_chunk(n):
        g = lookup([[r[n][0] for r in row] for row in chunks], z, y)
        first = unit_row(g, chunks[0][0][n][1])
        return pltpu.make_async_remote_copy(
            src_ref=int_hbm.at[
                pl.ds(pl.multiple_of(first - y * half_groups * 2 * unit, unit), unit), :
            ],
            dst_ref=int_scr.at[pl.ds(pl.multiple_of(first, unit), unit), :],
            send_sem=int_send.at[n],
            recv_sem=int_recv.at[n],
            device_id=y_peer,
            device_id_type=MESH,
        )

    n_chunks = 2 * half_groups

    own_copy = pltpu.make_async_copy(half_cols(y), block(z, x, c, y), own_sem.at[0])
    own_copy.start()
    kept = half_groups * 2 * unit
    held = pltpu.make_async_copy(
        int_hbm, int_scr.at[pl.ds(pl.multiple_of(y * kept, unit), kept), :], own_sem.at[1]
    )
    held.start()

    slots = vir_here // TILE

    def prepare_masks():
        for one in small:
            one.wait()
        lane = lax.broadcasted_iota(jnp.int32, (1, vir_here), 1) // TILE
        tile_of = jnp.zeros((1, vir_here), jnp.int32)
        for j in range(slots):
            tile_of = jnp.where(lane == j, owner_ref[w * slots + j], tile_of)
        q_tiles = imask_ref.shape[1]
        pick = lax.broadcasted_iota(jnp.int32, (q_tiles, vir_here), 0) == tile_of
        imask[...] = jnp.dot(
            imask_ref[...].astype(jnp.float32).astype(jnp.bfloat16),
            jnp.where(pick, 1.0, 0.0).astype(jnp.bfloat16),
            preferred_element_type=jnp.float32,
        )
        p_tiles = amask_ref.shape[1]
        p_lane = lax.broadcasted_iota(jnp.int32, (p_tiles, occ_here), 1) // TILE
        p_tile = y * (occ_here // TILE) + p_lane
        pick_p = lax.broadcasted_iota(jnp.int32, (p_tiles, occ_here), 0) == p_tile
        amask[...] = jnp.dot(
            amask_ref[...].astype(jnp.float32).astype(jnp.bfloat16),
            jnp.where(pick_p, 1.0, 0.0).astype(jnp.bfloat16),
            preferred_element_type=jnp.float32,
        )

    low = lax.broadcasted_iota(jnp.int32, (1, LANES), 1) < TILE

    def energies(tile, upper):
        row = vir_ref[pl.ds(tile // 2, 1), :]
        swapped = jnp.concatenate([row[:, TILE:], row[:, :TILE]], axis=1)
        odd = jnp.full((1, LANES), tile % 2, jnp.int32) == upper
        return jnp.where(odd, row, swapped)

    def prepare_reciprocals():
        occ_t = jnp.transpose(occ_ref[...])
        for j in range(occ_here // LANES):
            occ_cols[j * LANES : (j + 1) * LANES, :] = jnp.broadcast_to(
                occ_t[:, j : j + 1], (LANES, LANES)
            )
        for j in range(slots // 2):
            first = energies(owner_ref[w * slots + 2 * j], 0)
            second = energies(owner_ref[w * slots + 2 * j + 1], 1)
            vir_row = jnp.where(low, first, second)

            @pl.loop(0, occ_here // LANES)
            def _(i):
                at = pl.ds(pl.multiple_of(i * LANES, LANES), LANES)
                recip[at, j * LANES : (j + 1) * LANES] = 1.0 / (vir_row - occ_cols[at, :])

    step = 256

    def multiply(i):
        g = lookup([[r[i][2] for r in row] for row in units], z, y)
        far = lookup([[r[i][3] for r in row] for row in units], z, y)
        first_row = unit_row(g, far)
        xx = x + far - 2 * x * far
        for h in range(2):
            arrived(g, xx, 1 - c, h)

        tiles = unit // TILE
        last = i == 2 * z_count - 1

        def masked_amplitudes(cols):
            parts = []
            for t in range(tiles):
                at = pl.ds(pl.multiple_of(first_row + t * TILE, TILE), TILE)
                row = amask[pl.ds(first_row // TILE + t, 1), cols].astype(jnp.bfloat16)
                parts.append(amp_scr[at, cols] * jnp.broadcast_to(row, (TILE, step)))
            return jnp.concatenate(parts, axis=0)

        if last:
            for p in range(occ_here // step):
                cols = pl.ds(p * step, step)
                turned[cols, :] = jnp.transpose(masked_amplitudes(cols))

        order = [[r[i][4] for r in row] for row in units]
        here = int_scr.at[pl.ds(pl.multiple_of(first_row, unit), unit), :]
        for n in range(n_chunks):
            if any(n in row for row in order):

                @pl.when(lookup(order, z, y) == n)
                def _():
                    pltpu.make_async_remote_copy(
                        src_ref=here,
                        dst_ref=here,
                        send_sem=int_send.at[n],
                        recv_sem=int_recv.at[n],
                        device_id=y_peer,
                        device_id_type=MESH,
                    ).wait_recv()

        for t in range(tiles):
            at = pl.ds(pl.multiple_of(first_row + t * TILE, TILE), TILE)
            row = imask[pl.ds(first_row // TILE + t, 1), :].astype(jnp.bfloat16)
            int_scr[at, :] = int_scr[at, :] * jnp.broadcast_to(row, (TILE, vir_here))

        if last:
            right = int_scr[pl.ds(pl.multiple_of(first_row, unit), unit), :]
            for p in range(occ_here // step):
                cols = pl.ds(p * step, step)
                term = jnp.dot(turned[cols, :], right, preferred_element_type=jnp.float32)
                out_ref[cols, :] = ((acc[cols, :] + term) * recip[cols, :]).astype(jnp.bfloat16)
            return

        @pl.loop(0, occ_here // step)
        def _(p):
            cols = pl.ds(pl.multiple_of(p * step, step), step)
            term = lax.dot_general(
                masked_amplitudes(cols),
                int_scr[pl.ds(pl.multiple_of(first_row, unit), unit), :],
                (((0,), (0,)), ((), ())),
                preferred_element_type=jnp.float32,
            )
            if i == 0:
                acc[cols, :] = term
            else:
                acc[cols, :] += term

    def each_side(dist, act):
        if dist == 0:
            act(z, None)
            return

        @pl.when(z - dist >= 0)
        def _():
            act(z - dist, RIGHT)

        @pl.when(z + dist <= z_count - 1)
        def _():
            act(z + dist, LEFT)

    def arrival(kind, h, dist):
        along = h is own_half

        def from_end(zz, onward):
            return zz == (0 if onward == RIGHT else z_count - 1)

        def hand_on(zz, onward):
            @pl.when(has_r if onward == RIGHT else has_l)
            def _():
                copy(onward, zz, x, h).start()

        def from_z(zz, onward):
            arrived(zz, x, c, h)
            if not (along and dist == 2):
                hand_on(zz, onward)

            if along and dist >= 2:

                @pl.when(jnp.logical_not(from_end(zz, onward)))
                def _():
                    copy(ACROSS, zz, x, h).start()
            else:
                copy(ACROSS, zz, x, h).start()
            copy(CORE, zz, x, h).start()

        def from_x(zz, onward):
            arrived(zz, 1 - x, c, h)
            if along and 1 <= dist < z_count - 1:

                @pl.when(from_end(zz, onward))
                def _():
                    copy(RIGHT2 if onward == RIGHT else LEFT2, zz, 1 - x, h).start()

            copy(CORE2, zz, 1 - x, h).start()

        if kind == "y":
            arrived(z, x, c, h)
            spread_own(h, block(z, x, c, h))
        else:
            each_side(dist, {"z": from_z, "late": hand_on, "x": from_x}[kind])

    own_half, other_half = y, 1 - y
    prepare_masks()
    int_chunk(0).start()
    sent = 1
    for at, (kind, crossed, dist, when) in enumerate(ARRIVALS):
        arrival(kind, other_half if crossed else own_half, dist)
        if kind == "y":
            prepare_reciprocals()
        while sent < n_chunks and when >= 5.2 * (sent - 1) + 4.0:
            if sent >= 2:
                int_chunk(sent - 2).wait_send()
            int_chunk(sent).start()
            sent += 1
        for i in range(2 * z_count):
            if place[i] == at:
                if i == 0:
                    own_copy.wait()
                    held.wait()
                multiply(i)

    cross.wait_send()
    for n in range(n_chunks - 2, n_chunks):
        int_chunk(n).wait_send()
    for zz in range(z_count):
        for h in range(2):

            @pl.when(has_r & (zz <= z))
            def _():
                copy(RIGHT, zz, x, h).wait_send()

            @pl.when(has_l & (zz >= z))
            def _():
                copy(LEFT, zz, x, h).wait_send()

            around = False
            if zz == 0:
                around = (h == own_half) & (z >= 2)
            elif zz == z_count - 1:
                around = (h == own_half) & (z <= z_count - 3)
            if around is False:
                copy(ACROSS, zz, x, h).wait_send()
            else:

                @pl.when(jnp.logical_not(around))
                def _():
                    copy(ACROSS, zz, x, h).wait_send()

            copy(CORE, zz, x, h).wait_send()
            copy(CORE2, zz, 1 - x, h).wait_send()

    @pl.when(has_r & has_l)
    def _():
        copy(RIGHT2, 0, 1 - x, own_half).wait_send()
        copy(LEFT2, z_count - 1, 1 - x, own_half).wait_send()


def relayed(amplitudes, amp_mask, integrals, int_mask, owner, occ_energy, vir_energy):
    z_count = lax.axis_size("wide") // 4
    k_total = amplitudes.shape[0] * lax.axis_size("wide") * 2
    occ_here, vir_here = occ_energy.shape[0], integrals.shape[1]
    hbm = pl.BlockSpec(memory_space=pltpu.HBM)
    dma = pltpu.SemaphoreType.DMA
    occ_rows, vir_rows = occ_here // LANES, vir_energy.shape[0] // LANES
    return pl.pallas_call(
        functools.partial(ladder_kernel, z_count),
        out_shape=jax.ShapeDtypeStruct((occ_here, vir_here), jnp.bfloat16),
        in_specs=[hbm] * 7,
        out_specs=pl.BlockSpec(memory_space=pltpu.VMEM),
        scratch_shapes=[
            pltpu.VMEM((k_total, occ_here), jnp.bfloat16),
            pltpu.VMEM((k_total, vir_here), jnp.bfloat16),
            pltpu.VMEM((occ_here, vir_here), jnp.float32),
            pltpu.VMEM((occ_here, vir_here), jnp.float32),
            pltpu.VMEM((k_total // TILE, occ_here), jnp.float32),
            pltpu.VMEM((k_total // TILE, vir_here), jnp.float32),
            pltpu.VMEM((occ_here, LANES), jnp.float32),
            pltpu.VMEM(amp_mask.shape, jnp.int32),
            pltpu.VMEM(int_mask.shape, jnp.int32),
            pltpu.SMEM(owner.shape, jnp.int32),
            pltpu.VMEM((occ_rows, LANES), jnp.float32),
            pltpu.VMEM((vir_rows, LANES), jnp.float32),
            pltpu.VMEM((occ_here, k_total // (2 * z_count)), jnp.bfloat16),
            dma((7,)),
            dma,
            dma((z_count,)),
            dma((z_count,)),
            dma((7, 2 * z_count)),
            dma((8 * z_count,)),
        ],
        compiler_params=pltpu.CompilerParams(
            collective_id=0, has_side_effects=True, vmem_limit_bytes=40 * 2**20
        ),
        cost_estimate=pl.CostEstimate(
            flops=2 * k_total * occ_here * vir_here, bytes_accessed=4 * 2**20, transcendentals=0
        ),
    )(
        *(
            pltpu.with_memory_space_constraint(one, pltpu.HBM)
            for one in (
                amplitudes,
                integrals,
                amp_mask,
                int_mask,
                owner,
                occ_energy.reshape(-1, LANES),
                vir_energy.reshape(-1, LANES),
            )
        )
    )


def fits(mesh, amplitudes, integrals):
    wide, narrow = mesh.shape["wide"], mesh.shape["narrow"]
    return (
        narrow == 2
        and wide == 16
        and amplitudes.shape[0] == wide * narrow * TILE
        and amplitudes.shape[1] % (2 * 1024) == 0
        and (integrals.shape[1] // wide) % LANES == 0
    )


def solution(mesh):
    def run(amplitudes, amp_mask, integrals, int_mask, owner, occ_energy, vir_energy):
        body = relayed if fits(mesh, amplitudes, integrals) else shards
        return jax.shard_map(
            body,
            mesh=mesh,
            in_specs=(
                P(("wide", "narrow"), None),
                P(),
                P("narrow", "wide"),
                P(),
                P(),
                P("narrow"),
                P(),
            ),
            out_specs=P("narrow", "wide"),
            check_vma=False,
        )(amplitudes, amp_mask, integrals, int_mask, owner, occ_energy, vir_energy)

    return run
```

```python
import functools

import jax
import jax.numpy as jnp
from jax import lax
from jax.experimental import pallas as pl
from jax.experimental.pallas import tpu as pltpu
from jax.sharding import PartitionSpec as P

TILE = 64


def contract_rows(summed, rows_in, int_part):
    return summed + lax.dot_general(
        rows_in, int_part, (((0,), (0,)), ((), ())), preferred_element_type=jnp.float32
    )


def contract_all(amp_full, int_full, starting):
    k_total = amp_full.shape[0]
    block_rows = min(512, k_total)
    summed = starting
    for first_row in range(0, k_total, block_rows):
        summed = contract_rows(
            summed,
            amp_full[first_row : first_row + block_rows],
            int_full[first_row : first_row + block_rows],
        )
    return summed


def shards(amplitudes, amp_mask, integrals, int_mask, owner, occ_energy, vir_energy):
    tile_width = TILE
    narrow_count = lax.axis_size("narrow")
    wide_index = lax.axis_index("wide")
    narrow_index = lax.axis_index("narrow")
    src_rows = amplitudes.shape[0]
    occ_all = amplitudes.shape[1]
    occ_here = occ_energy.shape[0]
    vir_here = integrals.shape[1]
    first_src = (wide_index * narrow_count + narrow_index) * src_rows
    src_tiles = (first_src + jnp.arange(src_rows, dtype=jnp.int32)) // tile_width
    src_mask = jnp.take(amp_mask, src_tiles, axis=0)
    src_wide = jnp.broadcast_to(
        src_mask[:, :, None], (src_rows, occ_all // tile_width, tile_width)
    ).reshape(src_rows, occ_all)
    masked = jnp.where(src_wide == 1, amplitudes, jnp.zeros((), amplitudes.dtype))
    vir_tiles_here = vir_here // tile_width
    slot_ids = wide_index * vir_tiles_here + jnp.arange(vir_tiles_here, dtype=jnp.int32)
    tile_ids = jnp.take(owner, slot_ids)
    vir_mask = jnp.take(int_mask, tile_ids, axis=1)
    int_rows = integrals.shape[0]
    row_tiles = int_rows // tile_width
    local_mask = lax.dynamic_slice_in_dim(vir_mask, narrow_index * row_tiles, row_tiles, 0)
    local_wide = jnp.broadcast_to(
        local_mask[:, None, :, None], (row_tiles, tile_width, vir_tiles_here, tile_width)
    ).reshape(int_rows, vir_here)
    int_masked = jnp.where(local_wide == 1, integrals, jnp.zeros((), integrals.dtype))
    int_full = lax.all_gather(int_masked, "narrow", axis=0, tiled=True)
    starting = jnp.zeros((occ_here, vir_here), jnp.float32)
    regrouped = lax.all_to_all(masked, "narrow", split_axis=1, concat_axis=0, tiled=True)
    amp_full = lax.all_gather(regrouped, "wide", axis=0, tiled=True)
    ladder = contract_all(amp_full, int_full, starting)
    vir_energy_here = jnp.take(vir_energy.reshape(-1, tile_width), tile_ids, axis=0).reshape(
        vir_here
    )
    denominator = vir_energy_here[None, :] - occ_energy[:, None]
    return (ladder / denominator).astype(jnp.bfloat16)


MESH = pl.DeviceIdType.MESH
LANES = 128


def lookup(table, z, y):
    value = jnp.int32(table[0][0])
    for zz in range(len(table)):
        for yy in range(2):
            if table[zz][yy] != table[0][0]:
                value = jnp.where((z == zz) & (y == yy), jnp.int32(table[zz][yy]), value)
    return value


ARRIVALS = (
    ("z", 0, 1, 3.5),
    ("x", 0, 0, 3.5),
    ("y", 1, 0, 5.5),
    ("z", 0, 2, 6.5),
    ("x", 0, 1, 7.0),
    ("z", 1, 1, 9.0),
    ("x", 1, 0, 9.5),
    ("z", 0, 3, 10.0),
    ("z", 1, 2, 12.0),
    ("x", 0, 2, 12.0),
    ("x", 1, 1, 14.5),
    ("z", 1, 3, 16.0),
    ("x", 0, 3, 18.0),
    ("x", 1, 2, 18.5),
    ("x", 1, 3, 20.5),
)


def schedule(z_count):
    half = z_count // 2
    event = {(kind, dist): i for i, (kind, cross, dist, _) in enumerate(ARRIVALS) if cross == 1}
    event["z", 0] = event["y", 0]
    chunks = [[None] * 2 for _ in range(z_count)]
    units = [[None] * 2 for _ in range(z_count)]
    place = [0] * (2 * z_count)
    for z in range(z_count):
        for y in range(2):
            groups = sorted(range(y * half, (y + 1) * half), key=lambda g: abs(g - z))
            chunks[z][y] = [(g, e) for g in groups for e in range(2)]
        for y in range(2):
            remote = chunks[z][1 - y]
            rows = []
            for g in range(z_count):
                for e in range(2):
                    at = event["xz"[1 - e], abs(g - z)]
                    n = remote.index((g, e)) if (g, e) in remote else -1
                    ready = max(ARRIVALS[at][3], 9.5 + 5.6 * n)
                    rows.append((ready, at, g, e, n))
            rows.sort()
            units[z][y] = rows
            for i, (ready, at, _, _, _) in enumerate(rows):
                late = [j for j, a in enumerate(ARRIVALS) if a[3] + 1.0 >= ready]
                place[i] = max(place[i], at, late[0] if late else len(ARRIVALS) - 1)
    for i in range(1, len(place)):
        place[i] = max(place[i], place[i - 1])
    return chunks, units, place


def ladder_kernel(
    z_count,
    amp_hbm,
    int_hbm,
    amask_hbm,
    imask_hbm,
    owner_hbm,
    occ_hbm,
    vir_hbm,
    out_ref,
    amp_scr,
    int_scr,
    acc,
    recip,
    amask,
    imask,
    occ_cols,
    amask_ref,
    imask_ref,
    owner_ref,
    occ_ref,
    vir_ref,
    turned,
    own_sem,
    ycross_send,
    int_send,
    int_recv,
    send_sem,
    recv_sem,
):
    w = lax.axis_index("wide")
    y = lax.axis_index("narrow")
    z, x, c = w // 4, (w // 2) % 2, w % 2
    rows = amp_hbm.shape[0]
    occ_here, vir_here = acc.shape
    unit = int_scr.shape[0] // (2 * z_count)
    half_groups = z_count // 2
    chunks, units, place = schedule(z_count)

    def wide_id(zz, xx, cc):
        return zz * 4 + xx * 2 + cc

    y_peer = (w, 1 - y)
    x_peer = (wide_id(z, 1 - x, c), y)
    c_peer = (wide_id(z, x, 1 - c), y)
    r_peer = (w + 4, y)
    l_peer = (w - 4, y)
    has_r, has_l = z < z_count - 1, z > 0

    barrier = pltpu.get_barrier_semaphore()
    for peer in (y_peer, x_peer, c_peer):
        pl.semaphore_signal(barrier, inc=1, device_id=peer, device_id_type=MESH)

    @pl.when(has_r)
    def _():
        pl.semaphore_signal(barrier, inc=1, device_id=r_peer, device_id_type=MESH)

    @pl.when(has_l)
    def _():
        pl.semaphore_signal(barrier, inc=1, device_id=l_peer, device_id_type=MESH)

    small = [
        pltpu.make_async_copy(src, dst, own_sem.at[2 + i])
        for i, (src, dst) in enumerate(
            (
                (amask_hbm, amask_ref),
                (imask_hbm, imask_ref),
                (owner_hbm, owner_ref),
                (occ_hbm, occ_ref),
                (vir_hbm, vir_ref),
            )
        )
    ]
    for one in small:
        one.start()

    pl.semaphore_wait(barrier, 3 + jnp.where(has_r, 1, 0) + jnp.where(has_l, 1, 0))

    def block_id(zz, xx, cc, h):
        return wide_id(zz, xx, cc) * 2 + h

    def block(zz, xx, cc, h):
        first = pl.multiple_of(block_id(zz, xx, cc, h) * rows, rows)
        return amp_scr.at[pl.ds(first, rows), :]

    def half_cols(yy):
        return amp_hbm.at[:, pl.ds(pl.multiple_of(yy * occ_here, LANES), occ_here)]

    RIGHT, LEFT, ACROSS, CORE, CORE2, RIGHT2, LEFT2 = range(7)
    peers = (r_peer, l_peer, x_peer, c_peer, c_peer, r_peer, l_peer)

    def copy(kind, zz, xx, h, src=None):
        there = block(zz, xx, c, h)
        return pltpu.make_async_remote_copy(
            src_ref=there if src is None else src,
            dst_ref=there,
            send_sem=send_sem.at[kind, zz * 2 + h],
            recv_sem=recv_sem.at[block_id(zz, xx, c, h)],
            device_id=peers[kind],
            device_id_type=MESH,
        )

    def arrived(zz, xx, cc, h):
        here = block(zz, xx, cc, h)
        pltpu.make_async_remote_copy(
            src_ref=here,
            dst_ref=here,
            send_sem=send_sem.at[CORE, zz * 2 + h],
            recv_sem=recv_sem.at[block_id(zz, xx, cc, h)],
            device_id=c_peer,
            device_id_type=MESH,
        ).wait_recv()

    cross = pltpu.make_async_remote_copy(
        src_ref=half_cols(1 - y),
        dst_ref=block(z, x, c, y),
        send_sem=ycross_send,
        recv_sem=recv_sem.at[block_id(z, x, c, y)],
        device_id=y_peer,
        device_id_type=MESH,
    )
    cross.start()

    def spread_own(h, src):
        @pl.when(has_r)
        def _():
            copy(RIGHT, z, x, h, src).start()

        @pl.when(has_l)
        def _():
            copy(LEFT, z, x, h, src).start()

        copy(ACROSS, z, x, h, src).start()
        copy(CORE, z, x, h, src).start()

    spread_own(y, half_cols(y))

    def unit_row(g, far):
        return (g * 2 + x + far - 2 * x * far) * unit

    def int_chunk(n):
        g = lookup([[r[n][0] for r in row] for row in chunks], z, y)
        first = unit_row(g, chunks[0][0][n][1])
        return pltpu.make_async_remote_copy(
            src_ref=int_hbm.at[
                pl.ds(pl.multiple_of(first - y * half_groups * 2 * unit, unit), unit), :
            ],
            dst_ref=int_scr.at[pl.ds(pl.multiple_of(first, unit), unit), :],
            send_sem=int_send.at[n],
            recv_sem=int_recv.at[n],
            device_id=y_peer,
            device_id_type=MESH,
        )

    n_chunks = 2 * half_groups

    own_copy = pltpu.make_async_copy(half_cols(y), block(z, x, c, y), own_sem.at[0])
    own_copy.start()
    kept = half_groups * 2 * unit
    held = pltpu.make_async_copy(
        int_hbm, int_scr.at[pl.ds(pl.multiple_of(y * kept, unit), kept), :], own_sem.at[1]
    )
    held.start()

    slots = vir_here // TILE

    def prepare_masks():
        for one in small:
            one.wait()
        lane = lax.broadcasted_iota(jnp.int32, (1, vir_here), 1) // TILE
        tile_of = jnp.zeros((1, vir_here), jnp.int32)
        for j in range(slots):
            tile_of = jnp.where(lane == j, owner_ref[w * slots + j], tile_of)
        q_tiles = imask_ref.shape[1]
        pick = lax.broadcasted_iota(jnp.int32, (q_tiles, vir_here), 0) == tile_of
        imask[...] = jnp.dot(
            imask_ref[...].astype(jnp.float32).astype(jnp.bfloat16),
            jnp.where(pick, 1.0, 0.0).astype(jnp.bfloat16),
            preferred_element_type=jnp.float32,
        )
        p_tiles = amask_ref.shape[1]
        p_lane = lax.broadcasted_iota(jnp.int32, (p_tiles, occ_here), 1) // TILE
        p_tile = y * (occ_here // TILE) + p_lane
        pick_p = lax.broadcasted_iota(jnp.int32, (p_tiles, occ_here), 0) == p_tile
        amask[...] = jnp.dot(
            amask_ref[...].astype(jnp.float32).astype(jnp.bfloat16),
            jnp.where(pick_p, 1.0, 0.0).astype(jnp.bfloat16),
            preferred_element_type=jnp.float32,
        )

    low = lax.broadcasted_iota(jnp.int32, (1, LANES), 1) < TILE

    def energies(tile, upper):
        row = vir_ref[pl.ds(tile // 2, 1), :]
        swapped = jnp.concatenate([row[:, TILE:], row[:, :TILE]], axis=1)
        odd = jnp.full((1, LANES), tile % 2, jnp.int32) == upper
        return jnp.where(odd, row, swapped)

    def prepare_reciprocals():
        occ_t = jnp.transpose(occ_ref[...])
        for j in range(occ_here // LANES):
            occ_cols[j * LANES : (j + 1) * LANES, :] = jnp.broadcast_to(
                occ_t[:, j : j + 1], (LANES, LANES)
            )
        for j in range(slots // 2):
            first = energies(owner_ref[w * slots + 2 * j], 0)
            second = energies(owner_ref[w * slots + 2 * j + 1], 1)
            vir_row = jnp.where(low, first, second)

            @pl.loop(0, occ_here // LANES)
            def _(i):
                at = pl.ds(pl.multiple_of(i * LANES, LANES), LANES)
                recip[at, j * LANES : (j + 1) * LANES] = 1.0 / (vir_row - occ_cols[at, :])

    step = 256

    def multiply(i):
        g = lookup([[r[i][2] for r in row] for row in units], z, y)
        far = lookup([[r[i][3] for r in row] for row in units], z, y)
        first_row = unit_row(g, far)
        xx = x + far - 2 * x * far
        for h in range(2):
            arrived(g, xx, 1 - c, h)

        tiles = unit // TILE
        last = i == 2 * z_count - 1

        def masked_amplitudes(cols):
            parts = []
            for t in range(tiles):
                at = pl.ds(pl.multiple_of(first_row + t * TILE, TILE), TILE)
                row = amask[pl.ds(first_row // TILE + t, 1), cols].astype(jnp.bfloat16)
                parts.append(amp_scr[at, cols] * jnp.broadcast_to(row, (TILE, step)))
            return jnp.concatenate(parts, axis=0)

        if last:
            for p in range(occ_here // step):
                cols = pl.ds(p * step, step)
                turned[cols, :] = jnp.transpose(masked_amplitudes(cols))

        order = [[r[i][4] for r in row] for row in units]
        here = int_scr.at[pl.ds(pl.multiple_of(first_row, unit), unit), :]
        for n in range(n_chunks):
            if any(n in row for row in order):

                @pl.when(lookup(order, z, y) == n)
                def _():
                    pltpu.make_async_remote_copy(
                        src_ref=here,
                        dst_ref=here,
                        send_sem=int_send.at[n],
                        recv_sem=int_recv.at[n],
                        device_id=y_peer,
                        device_id_type=MESH,
                    ).wait_recv()

        for t in range(tiles):
            at = pl.ds(pl.multiple_of(first_row + t * TILE, TILE), TILE)
            row = imask[pl.ds(first_row // TILE + t, 1), :].astype(jnp.bfloat16)
            int_scr[at, :] = int_scr[at, :] * jnp.broadcast_to(row, (TILE, vir_here))

        if last:
            right = int_scr[pl.ds(pl.multiple_of(first_row, unit), unit), :]
            for p in range(occ_here // step):
                cols = pl.ds(p * step, step)
                term = jnp.dot(turned[cols, :], right, preferred_element_type=jnp.float32)
                out_ref[cols, :] = ((acc[cols, :] + term) * recip[cols, :]).astype(jnp.bfloat16)
            return

        @pl.loop(0, occ_here // step)
        def _(p):
            cols = pl.ds(pl.multiple_of(p * step, step), step)
            term = lax.dot_general(
                masked_amplitudes(cols),
                int_scr[pl.ds(pl.multiple_of(first_row, unit), unit), :],
                (((0,), (0,)), ((), ())),
                preferred_element_type=jnp.float32,
            )
            if i == 0:
                acc[cols, :] = term
            else:
                acc[cols, :] += term

    def each_side(dist, act):
        if dist == 0:
            act(z, None)
            return

        @pl.when(z - dist >= 0)
        def _():
            act(z - dist, RIGHT)

        @pl.when(z + dist <= z_count - 1)
        def _():
            act(z + dist, LEFT)

    def arrival(kind, h, dist):
        along = h is own_half

        def from_end(zz, onward):
            return zz == (0 if onward == RIGHT else z_count - 1)

        def from_z(zz, onward):
            arrived(zz, x, c, h)

            @pl.when(has_r if onward == RIGHT else has_l)
            def _():
                copy(onward, zz, x, h).start()

            if along and dist >= 2:

                @pl.when(jnp.logical_not(from_end(zz, onward)))
                def _():
                    copy(ACROSS, zz, x, h).start()
            else:
                copy(ACROSS, zz, x, h).start()
            copy(CORE, zz, x, h).start()

        def from_x(zz, onward):
            arrived(zz, 1 - x, c, h)
            if along and 1 <= dist < z_count - 1:

                @pl.when(from_end(zz, onward))
                def _():
                    copy(RIGHT2 if onward == RIGHT else LEFT2, zz, 1 - x, h).start()

            copy(CORE2, zz, 1 - x, h).start()

        if kind == "y":
            arrived(z, x, c, h)
            spread_own(h, block(z, x, c, h))
        else:
            each_side(dist, from_z if kind == "z" else from_x)

    own_half, other_half = y, 1 - y
    prepare_masks()
    int_chunk(0).start()
    sent = 1
    for at, (kind, crossed, dist, when) in enumerate(ARRIVALS):
        arrival(kind, other_half if crossed else own_half, dist)
        if kind == "y":
            prepare_reciprocals()
        while sent < n_chunks and when >= 5.2 * (sent - 1) + 4.0:
            if sent >= 2:
                int_chunk(sent - 2).wait_send()
            int_chunk(sent).start()
            sent += 1
        for i in range(2 * z_count):
            if place[i] == at:
                if i == 0:
                    own_copy.wait()
                    held.wait()
                multiply(i)

    cross.wait_send()
    for n in range(n_chunks - 2, n_chunks):
        int_chunk(n).wait_send()
    for zz in range(z_count):
        for h in range(2):

            @pl.when(has_r & (zz <= z))
            def _():
                copy(RIGHT, zz, x, h).wait_send()

            @pl.when(has_l & (zz >= z))
            def _():
                copy(LEFT, zz, x, h).wait_send()

            around = False
            if zz == 0:
                around = (h == own_half) & (z >= 2)
            elif zz == z_count - 1:
                around = (h == own_half) & (z <= z_count - 3)
            if around is False:
                copy(ACROSS, zz, x, h).wait_send()
            else:

                @pl.when(jnp.logical_not(around))
                def _():
                    copy(ACROSS, zz, x, h).wait_send()

            copy(CORE, zz, x, h).wait_send()
            copy(CORE2, zz, 1 - x, h).wait_send()

    @pl.when(has_r & has_l)
    def _():
        copy(RIGHT2, 0, 1 - x, own_half).wait_send()
        copy(LEFT2, z_count - 1, 1 - x, own_half).wait_send()


def relayed(amplitudes, amp_mask, integrals, int_mask, owner, occ_energy, vir_energy):
    z_count = lax.axis_size("wide") // 4
    k_total = amplitudes.shape[0] * lax.axis_size("wide") * 2
    occ_here, vir_here = occ_energy.shape[0], integrals.shape[1]
    hbm = pl.BlockSpec(memory_space=pltpu.HBM)
    dma = pltpu.SemaphoreType.DMA
    occ_rows, vir_rows = occ_here // LANES, vir_energy.shape[0] // LANES
    return pl.pallas_call(
        functools.partial(ladder_kernel, z_count),
        out_shape=jax.ShapeDtypeStruct((occ_here, vir_here), jnp.bfloat16),
        in_specs=[hbm] * 7,
        out_specs=pl.BlockSpec(memory_space=pltpu.VMEM),
        scratch_shapes=[
            pltpu.VMEM((k_total, occ_here), jnp.bfloat16),
            pltpu.VMEM((k_total, vir_here), jnp.bfloat16),
            pltpu.VMEM((occ_here, vir_here), jnp.float32),
            pltpu.VMEM((occ_here, vir_here), jnp.float32),
            pltpu.VMEM((k_total // TILE, occ_here), jnp.float32),
            pltpu.VMEM((k_total // TILE, vir_here), jnp.float32),
            pltpu.VMEM((occ_here, LANES), jnp.float32),
            pltpu.VMEM(amp_mask.shape, jnp.int32),
            pltpu.VMEM(int_mask.shape, jnp.int32),
            pltpu.SMEM(owner.shape, jnp.int32),
            pltpu.VMEM((occ_rows, LANES), jnp.float32),
            pltpu.VMEM((vir_rows, LANES), jnp.float32),
            pltpu.VMEM((occ_here, k_total // (2 * z_count)), jnp.bfloat16),
            dma((7,)),
            dma,
            dma((z_count,)),
            dma((z_count,)),
            dma((7, 2 * z_count)),
            dma((8 * z_count,)),
        ],
        compiler_params=pltpu.CompilerParams(
            collective_id=0, has_side_effects=True, vmem_limit_bytes=40 * 2**20
        ),
        cost_estimate=pl.CostEstimate(
            flops=2 * k_total * occ_here * vir_here, bytes_accessed=4 * 2**20, transcendentals=0
        ),
    )(
        *(
            pltpu.with_memory_space_constraint(one, pltpu.HBM)
            for one in (
                amplitudes,
                integrals,
                amp_mask,
                int_mask,
                owner,
                occ_energy.reshape(-1, LANES),
                vir_energy.reshape(-1, LANES),
            )
        )
    )


def fits(mesh, amplitudes, integrals):
    wide, narrow = mesh.shape["wide"], mesh.shape["narrow"]
    return (
        narrow == 2
        and wide == 16
        and amplitudes.shape[0] == wide * narrow * TILE
        and amplitudes.shape[1] % (2 * 1024) == 0
        and (integrals.shape[1] // wide) % LANES == 0
    )


def solution(mesh):
    def run(amplitudes, amp_mask, integrals, int_mask, owner, occ_energy, vir_energy):
        body = relayed if fits(mesh, amplitudes, integrals) else shards
        return jax.shard_map(
            body,
            mesh=mesh,
            in_specs=(
                P(("wide", "narrow"), None),
                P(),
                P("narrow", "wide"),
                P(),
                P(),
                P("narrow"),
                P(),
            ),
            out_specs=P("narrow", "wide"),
            check_vma=False,
        )(amplitudes, amp_mask, integrals, int_mask, owner, occ_energy, vir_energy)

    return run
```
